128 devices in a mesh: boxes: 128 (over x, z, y, core).
Axes of the slice: x: 4, y: 4, z: 4, core: 2. Of those that a mesh axis runs over, the one named last changes fastest.
Arguments:
- old_state: float32 [2048, 5, 4096], P('boxes'), may hold values from -6 to 6
- old_map: int32 [2048], replicated, may hold values from 0 to 2047, as said below
- new_map: int32 [2048], replicated, may hold values from 0 to 2047, as said below
- box_level: int32 [2048], replicated, may hold values from 0 to 1, as said below
- ghost_list: int32 [2048, 6, 4], replicated, may hold values from -1 to 2047, as said below
- coupling: float32 [3, 5, 5], replicated, may hold values from -2.5 to 2.5
Outputs:
- stepped: float32 [2048, 5, 4096], P('boxes')
The draws below stay inside these ranges and needn't reach their ends.
Inputs may be any that keep to these rules, and one draw needn't show every extreme that they name: A permutation: old slot s holds box old_map[s]. Each device sends exactly 1 of its boxes to each of 16 devices (itself possibly among them) and none to the others. A permutation: new slot t holds box new_map[t]. `box_level`: 1 for the fine boxes of the wall slab, half of all boxes; 0 for the coarse boxes. ghost_list[b, f] = (g, p, o1, o2): g is the source box or -1 at a wall, p lies in 0 to 15; where box_level[g] equals box_level[b], o1 = o2 = 0; otherwise box_level[g] = box_level[b] - 1 and o1, o2 are 0 or 8. The source of every ghost plane is owned under new_map by the target box's owner or by a device at most two indices away along the axis, counting around the end; at most 20 planes of one device are needed by another, a number reached in every draw.
All inputs are finite; a program needn't handle non-finite values.
Results may differ from the reference program's by a relative error of at most 0.0003.
Values sent between devices are 32-bit elements; how exact they have to be, the bound alone decides.
A program may use at most 256 MiB of HBM per device.

```python
import jax
import jax.numpy as jnp
import numpy as np
from jax import lax

F = 5
E = 16
CZB = 4
BOX_DEV = 16
NBOX = 2048
E3 = 4096
CAP = 1
N_BOXES = 128


def geometry(key):
    devices = NBOX // BOX_DEV
    fine_y = BOX_DEV // 2
    coarse_x = devices // 2
    coarse_y = BOX_DEV // 4
    half_y = coarse_y // 2
    fine_count = devices * fine_y
    fine_i, fine_j = np.meshgrid(np.arange(devices), np.arange(fine_y), indexing='ij')
    fine_i = fine_i.reshape(-1)
    fine_j = fine_j.reshape(-1)
    coarse_i, coarse_j, coarse_k = np.meshgrid(np.arange(coarse_x), np.arange(coarse_y), np.arange(CZB), indexing='ij')
    coarse_i = coarse_i.reshape(-1)
    coarse_j = coarse_j.reshape(-1)
    coarse_k = coarse_k.reshape(-1)

    def fine_index(first, second):
        return first % devices * fine_y + second % fine_y

    def coarse_index(first, second, third):
        return fine_count + (first % coarse_x * coarse_y + second % coarse_y) * CZB + third
    zeros_fine = fine_i * 0
    fine_rows = np.stack([np.stack([fine_index(fine_i - 1, fine_j), zeros_fine + E - 1, zeros_fine, zeros_fine], 1), np.stack([fine_index(fine_i + 1, fine_j), zeros_fine, zeros_fine, zeros_fine], 1), np.stack([fine_index(fine_i, fine_j - 1), zeros_fine + E - 1, zeros_fine, zeros_fine], 1), np.stack([fine_index(fine_i, fine_j + 1), zeros_fine, zeros_fine, zeros_fine], 1), np.stack([zeros_fine - 1, zeros_fine, zeros_fine, zeros_fine], 1), np.stack([coarse_index(fine_i // 2, fine_j // 2, 0), zeros_fine + E // 2, fine_i % 2 * (E // 2), fine_j % 2 * (E // 2)], 1)], 1)
    zeros_coarse = coarse_i * 0
    below = np.where(coarse_k > 0, coarse_index(coarse_i, coarse_j, coarse_k - 1), -1)
    above = np.where(coarse_k < CZB - 1, coarse_index(coarse_i, coarse_j, coarse_k + 1), -1)
    coarse_rows = np.stack([np.stack([coarse_index(coarse_i - 1, coarse_j, coarse_k), zeros_coarse + E - 1, zeros_coarse, zeros_coarse], 1), np.stack([coarse_index(coarse_i + 1, coarse_j, coarse_k), zeros_coarse, zeros_coarse, zeros_coarse], 1), np.stack([coarse_index(coarse_i, coarse_j - 1, coarse_k), zeros_coarse + E - 1, zeros_coarse, zeros_coarse], 1), np.stack([coarse_index(coarse_i, coarse_j + 1, coarse_k), zeros_coarse, zeros_coarse, zeros_coarse], 1), np.stack([below, np.where(coarse_k > 0, E - 1, 0), zeros_coarse, zeros_coarse], 1), np.stack([above, zeros_coarse, zeros_coarse, zeros_coarse], 1)], 1)
    table = np.concatenate([fine_rows, coarse_rows], 0).astype(np.int32)
    geo_device = np.concatenate([fine_i, 2 * coarse_i + coarse_j // half_y]).astype(np.int32)
    geo_local = np.concatenate([fine_j, fine_y + coarse_j % half_y * CZB + coarse_k]).astype(np.int32)
    fine_flag = np.concatenate([fine_i * 0 + 1, coarse_i * 0]).astype(np.int32)
    keys = jax.random.split(key, 5)
    label = jax.random.permutation(keys[0], NBOX).astype(jnp.int32)
    new_local = jax.vmap(lambda one: jax.random.permutation(one, BOX_DEV))(jax.random.split(keys[1], devices)).astype(jnp.int32)
    new_slot = jnp.asarray(geo_device) * BOX_DEV + new_local[jnp.asarray(geo_device), jnp.asarray(geo_local)]
    new_map = jnp.zeros((NBOX,), jnp.int32).at[new_slot].set(label)
    cycle = jax.random.permutation(keys[2], devices).astype(jnp.int32)
    cycle_inverse = jnp.zeros((devices,), jnp.int32).at[cycle].set(jnp.arange(devices, dtype=jnp.int32))
    offsets = jax.random.permutation(keys[3], devices).astype(jnp.int32)[:BOX_DEV // CAP]
    old_local = jax.vmap(lambda one: jax.random.permutation(one, BOX_DEV))(jax.random.split(keys[4], devices)).astype(jnp.int32)
    dest_grid, slot_grid = np.meshgrid(np.arange(devices), np.arange(BOX_DEV), indexing='ij')
    dest_grid = jnp.asarray(dest_grid.reshape(-1), jnp.int32)
    slot_grid = jnp.asarray(slot_grid.reshape(-1), jnp.int32)
    group = slot_grid // CAP
    source_device = cycle[(cycle_inverse[dest_grid] - offsets[group]) % devices]
    old_slot = source_device * BOX_DEV + old_local[source_device, group * CAP + slot_grid % CAP]
    old_map = jnp.zeros((NBOX,), jnp.int32).at[old_slot].set(new_map[dest_grid * BOX_DEV + slot_grid])
    level = jnp.zeros((NBOX,), jnp.int32).at[label].set(jnp.asarray(fine_flag))
    table_j = jnp.asarray(table)
    source_geo = table_j[:, :, 0]
    source_ids = jnp.where(source_geo >= 0, label[jnp.maximum(source_geo, 0)], -1).astype(jnp.int32)
    rows = jnp.concatenate([source_ids[:, :, None], table_j[:, :, 1:]], 2)
    ghost_list = jnp.zeros((NBOX, 6, 4), jnp.int32).at[label].set(rows)
    return (old_map, new_map, level, ghost_list)


def draw_old_map(key, part):
    return geometry(key)[0]


def draw_new_map(key, part):
    return geometry(key)[1]


def draw_box_level(key, part):
    return geometry(key)[2]


def draw_ghost_list(key, part):
    return geometry(key)[3]


def block_levels(rng, dims, cuts, least, top_value):
    level, own = 1.0, jax.random.fold_in(rng, 6)
    for axis_at, parts in cuts:
        steps = jnp.exp(jax.random.uniform(jax.random.fold_in(own, axis_at), (parts,), jnp.float32, least / len(cuts), top_value / len(cuts)))
        level = level * jnp.repeat(steps, dims[axis_at] // parts).reshape([-1 if axis == axis_at else 1 for axis in range(len(dims))])
    return level


def normal_values(own_key, shape, deviation, most, cuts=(), held_as=jnp.bfloat16):
    drawn = deviation * jax.random.normal(own_key, shape, jnp.float32)
    if cuts:
        drawn = drawn * block_levels(own_key, shape, cuts, -0.22, 0.18)
    return jnp.clip(drawn, -most, most).astype(held_as)


def setup_inputs(seed: int = 0) -> dict:
    seeds = jax.random.split(jax.random.key(seed), 7)
    old_state = normal_values(seeds[0], (NBOX, F, E3), 1.0, 6.0, ((0, 128),), jnp.float32)
    old_map = draw_old_map(jax.random.fold_in(seeds[6], 71), 0)
    new_map = draw_new_map(jax.random.fold_in(seeds[6], 71), 0)
    box_level = draw_box_level(jax.random.fold_in(seeds[6], 71), 0)
    ghost_list = draw_ghost_list(jax.random.fold_in(seeds[6], 71), 0)
    coupling = normal_values(seeds[5], (3, F, F), F ** -0.5, 2.5, (), jnp.float32)
    return {"old_state": old_state, "old_map": old_map, "new_map": new_map, "box_level": box_level, "ghost_list": ghost_list, "coupling": coupling}


diffusion_number = 0.12
advection_number = 0.25


def extract_plane(stack, slot, axis_id, plane_index, offset_first, offset_second, ratio):
    edge = stack.shape[2]
    along_first = stack[slot, :, plane_index, :, :]
    along_second = stack[slot, :, :, plane_index, :]
    along_third = stack[slot, :, :, :, plane_index]
    plane = jnp.where(axis_id == 0, along_first, jnp.where(axis_id == 1, along_second, along_third))
    counter = jnp.arange(edge, dtype=jnp.int32)
    first = (offset_first + counter // ratio).astype(jnp.int32)
    second = (offset_second + counter // ratio).astype(jnp.int32)
    return jnp.take(jnp.take(plane, first, axis=1), second, axis=2)


def mix_fields(matrix, field):
    return jnp.einsum("gf,fxyz->gxyz", matrix, field, precision=lax.Precision.HIGHEST)


def increment_from(padded, cells, scale, coupling):
    lower_first = padded[:, :-2, 1:-1, 1:-1]
    upper_first = padded[:, 2:, 1:-1, 1:-1]
    lower_second = padded[:, 1:-1, :-2, 1:-1]
    upper_second = padded[:, 1:-1, 2:, 1:-1]
    lower_third = padded[:, 1:-1, 1:-1, :-2]
    upper_third = padded[:, 1:-1, 1:-1, 2:]
    laplace = (upper_first + lower_first) + (upper_second + lower_second) + (upper_third + lower_third) - 6.0 * cells
    flux = mix_fields(coupling[0], upper_first - lower_first)
    flux = flux + mix_fields(coupling[1], upper_second - lower_second)
    flux = flux + mix_fields(coupling[2], upper_third - lower_third)
    return (diffusion_number / (scale * scale)) * laplace - (advection_number / scale) * 0.5 * flux


def stencil_step(cells, ghosts, scale, coupling):
    padded = jnp.pad(cells, ((0, 0), (1, 1), (1, 1), (1, 1)))
    padded = padded.at[:, 0, 1:-1, 1:-1].set(ghosts[0])
    padded = padded.at[:, -1, 1:-1, 1:-1].set(ghosts[1])
    padded = padded.at[:, 1:-1, 0, 1:-1].set(ghosts[2])
    padded = padded.at[:, 1:-1, -1, 1:-1].set(ghosts[3])
    padded = padded.at[:, 1:-1, 1:-1, 0].set(ghosts[4])
    padded = padded.at[:, 1:-1, 1:-1, -1].set(ghosts[5])
    return cells + increment_from(padded, cells, scale, coupling)


def reference(old_state, old_map, new_map, box_level, ghost_list, coupling):
    total = old_map.shape[0]
    fields = old_state.shape[1]
    slots = jnp.arange(total, dtype=jnp.int32)
    old_place = jnp.zeros((total,), jnp.int32).at[old_map].set(slots)
    stack = old_state.reshape(total, fields, E, E, E)

    def one_box(box_id):
        cells = stack[old_place[box_id]]
        level_here = box_level[box_id]
        entries = ghost_list[box_id]
        planes = []
        for face in range(6):
            source = entries[face, 0]
            source_id = jnp.maximum(source, 0).astype(jnp.int32)
            ratio = jnp.where(box_level[source_id] < level_here, 2, 1).astype(jnp.int32)
            plane = extract_plane(stack, old_place[source_id], face // 2, entries[face, 1], entries[face, 2], entries[face, 3], ratio)
            planes.append(jnp.where(source >= 0, plane, jnp.zeros_like(plane)))
        ghosts = jnp.stack(planes)
        scale = (2 - level_here).astype(jnp.float32)
        return stencil_step(cells, ghosts, scale, coupling).reshape(fields, E * E * E)

    def one_block(box_ids):
        return jax.vmap(one_box)(box_ids)

    stepped = lax.map(one_block, new_map.reshape(N_BOXES, BOX_DEV))
    return stepped.reshape(total, fields, E * E * E)
```

```python
import functools

import jax
import jax.numpy as jnp
from jax import lax
from jax.experimental import pallas as pl
from jax.experimental.pallas import tpu as pltpu

from jax.sharding import PartitionSpec as P

MESH = pl.DeviceIdType.MESH
N = 128
STRIDE = 37


def partner(me, k):
    return lax.rem(me + k * STRIDE, N)


def bytes_of(ref, sem):
    return pltpu.make_async_copy(ref, ref, sem)


def kernel(state, old_map, new_map, out, tiles, send_a, send_ar, recv_a, recv_ar, rolled, send_b, send_br,
           recv_br, cells, src_v, src_s, load_sem, send_sem, recv_sem, small_sem):
    me = lax.axis_index("boxes")
    barrier = pltpu.get_barrier_semaphore()

    def greet(k, c):
        pl.semaphore_signal(barrier, inc=1, device_id=(partner(me, k),), device_id_type=MESH)
        return c

    lax.fori_loop(1, N, greet, 0)

    def fetch(r, c):
        pltpu.make_async_copy(
            state.at[:, :, pl.ds(pl.multiple_of(r * 128, 128), 128)],
            tiles.at[pl.ds(r * 16, 16), pl.ds(0, 5), :],
            load_sem,
        ).start()
        return c

    lax.fori_loop(0, 32, fetch, 0)
    bytes_of(tiles.at[:, pl.ds(0, 5), :], load_sem).wait()
    rows = tiles.reshape(4096, 128)

    def pack(m):
        f = m // 32
        r = lax.rem(m, 32)
        return rows[pl.ds(r * 128 + f, 16, stride=8), :]

    pl.semaphore_wait(barrier, N - 1)

    def scatter(k, c):
        m = partner(me, k)
        send_a[m] = pack(m)
        pltpu.make_async_remote_copy(
            src_ref=send_a.at[m], dst_ref=recv_a.at[me], send_sem=send_sem.at[0], recv_sem=recv_sem.at[0],
            device_id=(m,), device_id_type=MESH,
        ).start()
        return c

    lax.fori_loop(1, N, scatter, 0)
    recv_a[me] = pack(me)

    def pack_rest(r, c):
        tile = rows[pl.ds(r * 128 + 4, 16, stride=8), :]
        for q in range(4):
            send_ar[r * 4 + q] = jnp.concatenate(
                [tile[4 * b:4 * b + 4, 32 * q:32 * q + 32] for b in range(4)], axis=1)
        return c

    lax.fori_loop(0, 32, pack_rest, 0)

    def scatter_rest(k, c):
        m = partner(me, k)
        pltpu.make_async_remote_copy(
            src_ref=send_ar.at[m], dst_ref=recv_ar.at[me], send_sem=send_sem.at[1], recv_sem=recv_sem.at[1],
            device_id=(m,), device_id_type=MESH,
        ).start()
        return c

    lax.fori_loop(1, N, scatter_rest, 0)
    recv_ar[me] = send_ar[me]

    wanted = new_map[...]

    def find(s, c):
        return jnp.where(wanted == old_map[s], s, c)

    source = lax.fori_loop(0, 2048, find, jnp.zeros((16, 128), jnp.int32), unroll=8)
    lane = lax.broadcasted_iota(jnp.int32, (16, 128), 1)
    turn = (lane // 4 - source // 4 + 8) % 4
    src_v[0:16] = source
    src_v[16:32] = turn * 512 + source // 16 * 4 + source % 4
    pltpu.make_async_copy(src_v, src_s, small_sem).start()
    pltpu.make_async_copy(src_v, src_s, small_sem).wait()

    bytes_of(recv_a.at[pl.ds(0, N - 1)], recv_sem.at[0]).wait()
    bytes_of(recv_ar.at[pl.ds(0, N - 1)], recv_sem.at[1]).wait()

    def turn_rest(s, c):
        piece = recv_ar[pl.ds(s * 4, 4)].reshape(16, 128)
        for t in range(4):
            rolled[pl.ds(pl.multiple_of(t * 512 + s * 16, 16), 16), :] = (
                pltpu.roll(piece, 32 * t, 1) if t else piece)
        return c

    lax.fori_loop(0, 32, turn_rest, 0)
    arrived = recv_a.reshape(2048, 128)
    quarter = lax.broadcasted_iota(jnp.int32, (1, 128), 1) // 32

    def gather(d, into, into_rest):
        hi = d // 8
        lo = lax.rem(d, 8) * 16
        for t in range(16):
            into(t, arrived[pl.ds(src_s[hi, lo + t], 1), :])
        for q in range(4):
            row = jnp.zeros((1, 128), jnp.float32)
            for i in range(4):
                row = jnp.where(quarter == i, rolled[pl.ds(src_s[16 + hi, lo + i * 4 + q], 1), :], row)
            into_rest(q, row)

    def forward(k, c):
        d = partner(me, k)

        def into(t, row):
            send_b[d, pl.ds(t, 1), :] = row

        def into_rest(q, row):
            send_br[d, pl.ds(q, 1), :] = row

        gather(d, into, into_rest)
        pltpu.make_async_remote_copy(
            src_ref=send_b.at[d], dst_ref=cells.at[me], send_sem=send_sem.at[2], recv_sem=recv_sem.at[2],
            device_id=(d,), device_id_type=MESH,
        ).start()
        pltpu.make_async_remote_copy(
            src_ref=send_br.at[d], dst_ref=recv_br.at[me], send_sem=send_sem.at[3], recv_sem=recv_sem.at[3],
            device_id=(d,), device_id_type=MESH,
        ).start()
        return c

    lax.fori_loop(1, N, forward, 0)

    def into_own(t, row):
        cells[me, pl.ds(t, 1), :] = row

    def into_own_rest(q, row):
        recv_br[me, pl.ds(q, 1), :] = row

    gather(me, into_own, into_own_rest)
    bytes_of(cells.at[pl.ds(0, N - 1)], recv_sem.at[2]).wait()
    bytes_of(recv_br.at[pl.ds(0, N - 1)], recv_sem.at[3]).wait()

    def unpack_rest(r, c):
        parts = [recv_br[r * 4 + q] for q in range(4)]
        for b in range(4):
            cells[128 + r, 4 * b:4 * b + 4, :] = jnp.concatenate(
                [part[:, 32 * b:32 * b + 32] for part in parts], axis=1)
        return c

    lax.fori_loop(0, 32, unpack_rest, 0)
    out[...] = cells[...]
    for at, ref in ((0, send_a), (1, send_ar), (2, send_b), (3, send_br)):
        bytes_of(ref.at[pl.ds(0, N - 1)], send_sem.at[at]).wait()


def regrid(state, old_map, new_map):
    vmem = pl.BlockSpec(memory_space=pltpu.VMEM)
    f32 = jnp.float32
    return pl.pallas_call(
        kernel,
        out_shape=jax.ShapeDtypeStruct((160, 16, 128), f32),
        in_specs=[pl.BlockSpec(memory_space=pl.ANY), pl.BlockSpec(memory_space=pltpu.SMEM), vmem],
        out_specs=vmem,
        scratch_shapes=[
            pltpu.VMEM((512, 8, 128), f32),
            pltpu.VMEM((N, 16, 128), f32),
            pltpu.VMEM((N, 4, 128), f32),
            pltpu.VMEM((N, 16, 128), f32),
            pltpu.VMEM((N, 4, 128), f32),
            pltpu.VMEM((2048, 128), f32),
            pltpu.VMEM((N, 16, 128), f32),
            pltpu.VMEM((N, 4, 128), f32),
            pltpu.VMEM((N, 4, 128), f32),
            pltpu.VMEM((160, 16, 128), f32),
            pltpu.VMEM((32, 128), jnp.int32),
            pltpu.SMEM((32, 128), jnp.int32),
            pltpu.SemaphoreType.DMA,
            pltpu.SemaphoreType.DMA((4,)),
            pltpu.SemaphoreType.DMA((4,)),
            pltpu.SemaphoreType.DMA,
        ],
        compiler_params=pltpu.CompilerParams(
            collective_id=0, has_side_effects=True, vmem_limit_bytes=48 << 20),
    )(state, old_map, new_map.reshape(16, 128))


E = 16
GCAP = 20


diffusion_number = 0.12
advection_number = 0.25


def shifted(value, axis, steps):
    count = lax.axis_size(axis)
    pairs = [(source, (source + steps) % count) for source in range(count)]
    return lax.ppermute(value, axis, pairs)


def mix_fields(matrix, field):
    return jnp.einsum("gf,fxyz->gxyz", matrix, field, precision=lax.Precision.HIGHEST)


def increment_from(padded, cells, scale, coupling):
    lower_first = padded[:, :-2, 1:-1, 1:-1]
    upper_first = padded[:, 2:, 1:-1, 1:-1]
    lower_second = padded[:, 1:-1, :-2, 1:-1]
    upper_second = padded[:, 1:-1, 2:, 1:-1]
    lower_third = padded[:, 1:-1, 1:-1, :-2]
    upper_third = padded[:, 1:-1, 1:-1, 2:]
    laplace = (
        upper_first
        + lower_first
        + (upper_second + lower_second)
        + (upper_third + lower_third)
        - 6.0 * cells
    )
    flux = mix_fields(coupling[0], upper_first - lower_first)
    flux = flux + mix_fields(coupling[1], upper_second - lower_second)
    flux = flux + mix_fields(coupling[2], upper_third - lower_third)
    return diffusion_number / (scale * scale) * laplace - advection_number / scale * 0.5 * flux


def surround(cells, ghosts):
    fields, edge = (cells.shape[0], cells.shape[1])
    inner = jnp.concatenate([ghosts[4][:, :, :, None], cells, ghosts[5][:, :, :, None]], 3)
    zero_third = jnp.zeros((fields, edge, 1), jnp.float32)
    lower_second = jnp.concatenate([zero_third, ghosts[2], zero_third], 2)[:, :, None, :]
    upper_second = jnp.concatenate([zero_third, ghosts[3], zero_third], 2)[:, :, None, :]
    inner = jnp.concatenate([lower_second, inner, upper_second], 2)
    lower_first = jnp.pad(ghosts[0], ((0, 0), (1, 1), (1, 1)))[:, None]
    upper_first = jnp.pad(ghosts[1], ((0, 0), (1, 1), (1, 1)))[:, None]
    return jnp.concatenate([lower_first, inner, upper_first], 1)


def stencil_step(cells, ghosts, scale, coupling):
    padded = surround(cells, ghosts)
    return cells + increment_from(padded, cells, scale, coupling)


def requests_of(receiver, new_map, new_place, box_level, ghost_list, per_device):
    boxes = lax.dynamic_slice_in_dim(new_map, receiver * per_device, per_device)
    entries = ghost_list[boxes]
    source = entries[:, :, 0]
    valid = source >= 0
    source_id = jnp.maximum(source, 0)
    holder_slot = new_place[source_id]
    ratio = jnp.where(box_level[source_id] < box_level[boxes][:, None], 2, 1).astype(jnp.int32)
    axis_id = jnp.broadcast_to(jnp.arange(6, dtype=jnp.int32) // 2, source.shape)
    return (
        valid.reshape(-1),
        (holder_slot // per_device).reshape(-1),
        (holder_slot % per_device).reshape(-1),
        axis_id.reshape(-1),
        entries[:, :, 1].reshape(-1),
        entries[:, :, 2].reshape(-1),
        entries[:, :, 3].reshape(-1),
        ratio.reshape(-1),
    )


def planes_for(flat_cells, wanted, picks, edge):
    volume = edge * edge * edge
    slot = wanted[2][picks]
    axis_id = wanted[3][picks][:, None, None]
    plane_index = wanted[4][picks][:, None, None]
    ratio = wanted[7][picks][:, None]
    counter = jnp.arange(edge, dtype=jnp.int32)[None, :]
    first = wanted[5][picks][:, None] + counter // ratio
    second = wanted[6][picks][:, None] + counter // ratio
    along_u = first[:, :, None]
    along_v = second[:, None, :]
    index_first = (plane_index * edge + along_u) * edge + along_v
    index_second = (along_u * edge + plane_index) * edge + along_v
    index_third = (along_u * edge + along_v) * edge + plane_index
    cell_index = jnp.where(
        axis_id == 0, index_first, jnp.where(axis_id == 1, index_second, index_third)
    )
    where_flat = slot[:, None, None] * volume + cell_index
    count = picks.shape[0]
    fields = flat_cells.shape[0]
    taken = flat_cells[:, where_flat.reshape(-1)]
    return taken.reshape(fields, count, edge, edge).transpose(1, 0, 2, 3)


def send_planes(planes, distance):
    return shifted(planes, "boxes", distance)


def shards(old_state, old_map, new_map, box_level, ghost_list, coupling):
    devices = lax.axis_size("boxes")
    device_index = lax.axis_index("boxes")
    per_device, fields, volume = old_state.shape
    edge = E
    total = old_map.shape[0]
    plane_room = GCAP
    requests = 6 * per_device
    slots = jnp.arange(total, dtype=jnp.int32)
    new_place = jnp.zeros((total,), jnp.int32).at[new_map].set(slots)
    own_boxes = lax.dynamic_slice_in_dim(new_map, device_index * per_device, per_device)
    own_scale = (2 - box_level[own_boxes]).astype(jnp.float32)
    moved = regrid(old_state, old_map, new_map).reshape(fields, 32, per_device, 128)
    regridded = moved.transpose(2, 0, 1, 3).reshape(per_device, fields, volume)
    cells = regridded.reshape(per_device, fields, edge, edge, edge)
    flat_cells = regridded.transpose(1, 0, 2).reshape(fields, per_device * volume)
    mine = requests_of(device_index, new_map, new_place, box_level, ghost_list, per_device)
    every_request = jnp.arange(requests, dtype=jnp.int32)
    local_planes = planes_for(flat_cells, mine, every_request, edge)
    local_used = mine[0] & (mine[1] == device_index)
    ghosts = jnp.where(local_used[:, None, None, None], local_planes, 0.0)
    for distance in (1, 2, -1, -2):
        receiver = (device_index + distance) % devices
        wanted = requests_of(receiver, new_map, new_place, box_level, ghost_list, per_device)
        chosen = wanted[0] & (wanted[1] == device_index)
        order_index = jnp.cumsum(chosen.astype(jnp.int32)) - 1
        slot_table = (
            jnp.full((plane_room,), requests, jnp.int32)
            .at[jnp.where(chosen, order_index, plane_room)]
            .set(every_request, mode="drop")
        )
        used = slot_table < requests
        planes = planes_for(flat_cells, wanted, jnp.minimum(slot_table, requests - 1), edge)
        planes = jnp.where(used[:, None, None, None], planes, 0.0).reshape(
            plane_room, fields, edge * edge
        )
        incoming = send_planes(planes, distance).reshape(plane_room, fields, edge, edge)
        sender = (device_index - distance) % devices
        taken = mine[0] & (mine[1] == sender)
        arrival_rank = jnp.clip(jnp.cumsum(taken.astype(jnp.int32)) - 1, 0, plane_room - 1)
        ghosts = ghosts + jnp.where(taken[:, None, None, None], incoming[arrival_rank], 0.0)
    ghosts = ghosts.reshape(per_device, 6, fields, edge, edge)
    stepped = jax.vmap(stencil_step, in_axes=(0, 0, 0, None))(cells, ghosts, own_scale, coupling)
    stepped = stepped.reshape(per_device, fields, volume)
    return stepped


def solution(mesh):
    return jax.shard_map(
        shards,
        mesh=mesh,
        in_specs=(P("boxes", None, None), P(), P(), P(), P(), P()),
        out_specs=P("boxes", None, None),
        check_vma=False,
    )
```

```python
import functools

import jax
import jax.numpy as jnp
from jax import lax
from jax.experimental import pallas as pl
from jax.experimental.pallas import tpu as pltpu
from jax.sharding import PartitionSpec as P

MESH = pl.DeviceIdType.MESH
N = 128
BOXES = 16
STRIDE = 37
DISTANCES = (-2, -1, 1, 2)
ROOM = 20
ROWS = 24
PITCH = 36
BLOCK = 10 * BOXES
diffusion_number = 0.12
advection_number = 0.25


def partner(me, k):
    return lax.rem(me + k * STRIDE, N)


def bytes_of(ref, sem):
    return pltpu.make_async_copy(ref, ref, sem)


def put(src, dst, send_sem, recv_sem, device):
    pltpu.make_async_remote_copy(
        src_ref=src, dst_ref=dst, send_sem=send_sem, recv_sem=recv_sem, device_id=(device,), device_id_type=MESH,
    ).start()


def iota(shape, axis):
    return lax.broadcasted_iota(jnp.int32, shape, axis)


def running_count(chosen):
    lane = iota(chosen.shape, 1)
    count = chosen.astype(jnp.int32)
    for step in (1, 2, 4, 8, 16, 32, 64):
        count = count + jnp.where(lane >= step, pltpu.roll(count, step, 1), 0)
    return count


def swap_bits(rows, unit, steps):
    lane = iota(rows[0].shape, 1)
    rows = list(rows)
    for step in steps:
        high = (lane // (unit * step)) % 2 == 1
        for at in range(len(rows)):
            if at & step:
                continue
            low_row, high_row = rows[at], rows[at + step]
            rows[at] = jnp.where(high, pltpu.roll(high_row, unit * step, 1), low_row)
            rows[at + step] = jnp.where(high, high_row, pltpu.roll(low_row, 128 - unit * step, 1))
    return rows


def kernel(state, old_map, new_map, new_lanes, box_level, ghost_list, coupling, out,
           rest, send_ar, recv_a, recv_ar, rolled, send_b, send_br, recv_br, cells, src_v, src_s,
           old_s, new_s, level_s, ghost_s, mix_s, new_v, face_code, level_v, table_v, table_s,
           planes, outbox, inbox, raw, raw_far, faces,
           load_sem, send_sem, recv_sem, small_sem, far_send, far_recv):
    me = lax.axis_index("boxes")
    barrier = pltpu.get_barrier_semaphore()

    def greet(k, c):
        pl.semaphore_signal(barrier, inc=1, device_id=(partner(me, k),), device_id_type=MESH)
        return c

    lax.fori_loop(1, N, greet, 0)
    loads = [
        pltpu.make_async_copy(state.at[4], rest, load_sem.at[0]),
        pltpu.make_async_copy(old_map, old_s, load_sem.at[1]),
        pltpu.make_async_copy(new_map, new_s, load_sem.at[2]),
        pltpu.make_async_copy(new_lanes, new_v, load_sem.at[3]),
        pltpu.make_async_copy(box_level, level_s, load_sem.at[4]),
        pltpu.make_async_copy(ghost_list, ghost_s, load_sem.at[5]),
        pltpu.make_async_copy(coupling, mix_s, load_sem.at[6]),
    ]
    for load in loads:
        load.start()

    def piece(m):
        return state.at[m // 32, :, pl.ds(pl.multiple_of(lax.rem(m, 32) * 128, 128), 128)]

    own = pltpu.make_async_copy(piece(me), recv_a.at[me], load_sem.at[7])
    own.start()
    pl.semaphore_wait(barrier, N - 1)

    def scatter(k, c):
        m = partner(me, k)
        put(piece(m), recv_a.at[me], send_sem.at[0], recv_sem.at[0], m)
        return c

    lax.fori_loop(1, N, scatter, 0)
    loads[0].wait()

    def pack_rest(r, c):
        tile = rest[:, pl.ds(pl.multiple_of(r * 128, 128), 128)]
        for q in range(4):
            send_ar[r * 4 + q] = jnp.concatenate(
                [tile[4 * b:4 * b + 4, 32 * q:32 * q + 32] for b in range(4)], axis=1)
        return c

    lax.fori_loop(0, 32, pack_rest, 0)

    def scatter_rest(k, c):
        m = partner(me, k)
        put(send_ar.at[m], recv_ar.at[me], send_sem.at[1], recv_sem.at[1], m)
        return c

    lax.fori_loop(1, N, scatter_rest, 0)
    recv_ar[me] = send_ar[me]
    for load in loads[1:]:
        load.wait()

    wanted = new_v[...]

    def find(s, c):
        return jnp.where(wanted == old_s[s], s, c)

    source = lax.fori_loop(0, 2048, find, jnp.zeros((16, 128), jnp.int32), unroll=8)
    lane = iota((16, 128), 1)
    turn = (lane // 4 - source // 4 + 8) % 4
    src_v[0:16] = source
    src_v[16:32] = turn * 512 + source // 16 * 4 + source % 4
    to_scalars = pltpu.make_async_copy(src_v, src_s, small_sem.at[0])
    to_scalars.start()

    row8, lane8 = iota((8, 128), 0), iota((8, 128), 1)
    row16 = iota((16, 128), 0)
    nothing = jnp.full((8, 128), -1, jnp.int32)
    zeros16 = jnp.zeros((16, 128), jnp.int32)

    def read_wishes(k, c):
        theirs, their_plane, ours, our_plane, level_here, codes = c
        for at, distance in enumerate(DISTANCES):
            b = new_s[lax.rem(me + distance + N, N) * BOXES + k]
            for f in range(6):
                here = (row8 == at) & (lane8 == f * 16 + k)
                theirs = jnp.where(here, ghost_s[f, 0, b], theirs)
                their_plane = jnp.where(here, ghost_s[f, 1, b], their_plane)
        b = new_s[me * BOXES + k]
        level = level_s[b]
        level_here = jnp.where(row16 == k, level, level_here)
        new_codes = []
        for f in range(6):
            here = lane8 == f * 16 + k
            g = ghost_s[f, 0, b]
            ours = jnp.where(here, g, ours)
            our_plane = jnp.where(here, ghost_s[f, 1, b], our_plane)
            coarser = (level_s[jnp.maximum(g, 0)] < level).astype(jnp.int32)
            code = ghost_s[f, 2, b] // 8 + ghost_s[f, 3, b] // 8 * 2 + coarser * 4
            new_codes.append(jnp.where(row16 == k, code, codes[f]))
        return theirs, their_plane, ours, our_plane, level_here, tuple(new_codes)

    theirs, their_plane, ours, our_plane, level_here, codes = lax.fori_loop(
        0, BOXES, read_wishes, (nothing, nothing, nothing, nothing, zeros16, (zeros16,) * 6))
    level_v[...] = level_here
    for f in range(6):
        face_code[f] = codes[f]

    def find_theirs(t, c):
        return jnp.where(theirs == new_s[me * BOXES + t], t, c)

    their_slot = lax.fori_loop(0, BOXES, find_theirs, nothing)

    def find_ours(t, c):
        return jnp.where(ours == new_s[lax.rem((me - 2 + N) * BOXES + t, N * BOXES)], t, c)

    our_slot = lax.fori_loop(0, 5 * BOXES, find_ours, nothing)
    axis = lane8 // 32
    chosen = their_slot >= 0
    count = running_count(chosen)
    base = (axis * 16 + their_plane) * BLOCK + their_slot
    table = jnp.zeros((8, 128), jnp.int32)
    for j in range(ROOM):
        first = jnp.sum(jnp.where(chosen & (count == j + 1), base, 0), axis=1, keepdims=True)
        table = jnp.where(lane8 == j, first, table)
    low = jnp.where(row8 == 4, 32, jnp.where(row8 >= 2, row8 * 16 + 16, row8 * 16))
    chosen = (our_slot >= low) & (our_slot < low + 16) & (row8 < 5)
    count = running_count(chosen)
    far_base = jnp.sum(
        jnp.where(chosen & (row8 < 4), row8 * (10 * ROWS) + count - 1 - 40 * ROWS, 0), axis=0, keepdims=True)
    near_base = jnp.sum(
        jnp.where(chosen & (row8 == 4), (axis * 16 + our_plane) * BLOCK + our_slot - 32 - 48 * BLOCK, 0),
        axis=0, keepdims=True)
    table = jnp.where(row8 == 4, far_base + 40 * ROWS, table)
    table = jnp.where(row8 == 5, near_base + 48 * BLOCK, table)
    table_v[...] = table
    to_table = pltpu.make_async_copy(table_v, table_s, small_sem.at[1])
    to_table.start()
    planes[48] = jnp.zeros((10, BOXES, 128), jnp.float32)
    inbox[4] = jnp.zeros((10, ROWS, 128), jnp.float32)
    to_scalars.wait()
    to_table.wait()

    own.wait()
    bytes_of(recv_a.at[pl.ds(0, N - 1)], recv_sem.at[0]).wait()
    bytes_of(recv_ar.at[pl.ds(0, N - 1)], recv_sem.at[1]).wait()

    def turn_rest(s, c):
        part = recv_ar[pl.ds(s * 4, 4)].reshape(16, 128)
        for t in range(4):
            rolled[pl.ds(pl.multiple_of(t * 512 + s * 16, 16), 16), :] = (
                pltpu.roll(part, 32 * t, 1) if t else part)
        return c

    lax.fori_loop(0, 32, turn_rest, 0)
    arrived = recv_a.reshape(2048, 128)
    quarter = iota((1, 128), 1) // 32
    landing = me // 32 * PITCH + 2 + lax.rem(me, 32)

    def gather(d, into, into_rest):
        hi = d // 8
        lo = lax.rem(d, 8) * 16
        for t in range(16):
            into(t, arrived[pl.ds(src_s[hi, lo + t], 1), :])
        for q in range(4):
            row = jnp.zeros((1, 128), jnp.float32)
            for i in range(4):
                row = jnp.where(quarter == i, rolled[pl.ds(src_s[16 + hi, lo + i * 4 + q], 1), :], row)
            into_rest(q, row)

    def forward(k, c):
        d = partner(me, k)

        def into(t, row):
            send_b[d, pl.ds(t, 1), :] = row

        def into_rest(q, row):
            send_br[d, pl.ds(q, 1), :] = row

        gather(d, into, into_rest)
        put(send_b.at[d], cells.at[landing], send_sem.at[2], recv_sem.at[2], d)
        put(send_br.at[d], recv_br.at[me], send_sem.at[3], recv_sem.at[3], d)
        return c

    lax.fori_loop(1, N, forward, 0)

    def into_own(t, row):
        cells[landing, pl.ds(t, 1), :] = row

    def into_own_rest(q, row):
        recv_br[me, pl.ds(q, 1), :] = row

    gather(me, into_own, into_own_rest)
    bytes_of(cells.at[pl.ds(0, N - 1)], recv_sem.at[2]).wait()
    bytes_of(recv_br.at[pl.ds(0, N - 1)], recv_sem.at[3]).wait()

    def unpack_rest(r, c):
        parts = [recv_br[r * 4 + q] for q in range(4)]
        for b in range(4):
            cells[4 * PITCH + 2 + r, 4 * b:4 * b + 4, :] = jnp.concatenate(
                [part[:, 32 * b:32 * b + 32] for part in parts], axis=1)
        return c

    lax.fori_loop(0, 32, unpack_rest, 0)

    def transpose_planes(at, c):
        f, half, b = at // 4, at // 2 % 2, pl.multiple_of(at % 2 * 8, 8)
        rows = [cells[f * PITCH + 2 + 2 * i + half, pl.ds(b, 8), :] for i in range(16)]
        for i in range(16):
            planes[i, 2 * f + half, pl.ds(b, 8), :] = rows[i]
        for upper in range(2):
            turned = swap_bits(rows[8 * upper:8 * upper + 8], 16, (4, 2, 1))
            for j in range(8):
                planes[16 + 8 * half + j, 2 * f + upper, pl.ds(b, 8), :] = turned[j]
        turned = swap_bits(rows, 1, (8, 4, 2, 1))
        for k in range(16):
            planes[32 + k, 2 * f + half, pl.ds(b, 8), :] = turned[k]
        return c

    lax.fori_loop(0, 20, transpose_planes, 0)
    plane_rows = planes.reshape(49 * BLOCK, 128)

    for at, distance in enumerate(DISTANCES):
        def fill(j, c, at=at):
            base = table_s[at, j]
            for h in range(10):
                outbox[at, h, pl.ds(j, 1), :] = plane_rows[pl.ds(base + h * BOXES, 1), :]
            return c

        lax.fori_loop(0, ROOM, fill, 0)
        put(outbox.at[at], inbox.at[3 - at], far_send.at[at], far_recv.at[3 - at],
            lax.rem(me + distance + N, N))

    def take_near(q, c):
        base = table_s[5, q]
        for h in range(10):
            raw[h, pl.ds(q, 1), :] = plane_rows[pl.ds(base + h * BOXES, 1), :]
        return c

    lax.fori_loop(0, 96, take_near, 0)
    for at in range(4):
        bytes_of(inbox.at[at], far_recv.at[at]).wait()
    inbox_rows = inbox.reshape(50 * ROWS, 128)

    def take_far(q, c):
        base = table_s[4, q]
        for h in range(10):
            raw_far[h, pl.ds(q, 1), :] = inbox_rows[pl.ds(base + h * ROWS, 1), :]
        return c

    lax.fori_loop(0, 96, take_far, 0)

    lane = iota((16, 128), 1)
    for face in range(6):
        code = face_code[face]
        coarse = code >= 4
        first, second = code % 2, code // 2 % 2
        if face >= 4:
            first, second = second, first
        picks = [
            jnp.where(coarse, (4 * half + lane // 32) * 16 + 8 * second + lane % 16 // 2, lane)
            for half in range(2)
        ]
        low_first = coarse & (first == 0)
        high_first = coarse & (first == 1)

        def refine(f, c, face=face, picks=picks, low_first=low_first, high_first=high_first):
            part = [raw[2 * f + h, 16 * face:16 * face + 16, :] + raw_far[2 * f + h, 16 * face:16 * face + 16, :]
                    for h in range(2)]
            chosen = [jnp.where(high_first, part[1], part[0]), jnp.where(low_first, part[0], part[1])]
            for h in range(2):
                value = jnp.take_along_axis(chosen[h], picks[h], axis=1, mode="promise_in_bounds")
                if face < 2:
                    cells[f * PITCH + 34 * face + h] = value
                else:
                    faces[face - 2, 2 * f + h] = value
            return c

        lax.fori_loop(0, 5, refine, 0)

    lane = iota((8, 128), 1)
    third = lane % 16

    def step(at, c):
        i, b = at // 2, pl.multiple_of(at % 2 * 8, 8)
        eighth = lax.rem(i, 8)
        scale = (2 - level_v[pl.ds(b, 8), :]).astype(jnp.float32)
        spread = diffusion_number / (scale * scale)
        drift = advection_number / scale * 0.5

        def at_row(f, r):
            return cells[f * PITCH + 2 + r, pl.ds(b, 8), :]

        values = [[at_row(f, 2 * i + h) for h in range(2)] for f in range(5)]
        for half in range(2):
            sums, differences = [], []
            for f in range(5):
                here, other = values[f][half], values[f][1 - half]
                before, after = at_row(f, 2 * i + half - 2), at_row(f, 2 * i + half + 2)
                total = after + before - 6.0 * here
                moves = [after - before]
                if half == 0:
                    edge = pltpu.roll(
                        faces[0, 2 * f + i // 8, pl.ds(b, 8), :], lax.rem(128 - eighth * 16, 128), 1)
                    before = jnp.where(lane < 16, edge, pltpu.roll(here, 16, 1))
                    after = pltpu.roll(jnp.where(lane < 16, other, here), 112, 1)
                else:
                    edge = pltpu.roll(faces[1, 2 * f + i // 8, pl.ds(b, 8), :], 112 - eighth * 16, 1)
                    before = pltpu.roll(jnp.where(lane >= 112, other, here), 16, 1)
                    after = jnp.where(lane >= 112, edge, pltpu.roll(here, 112, 1))
                total = total + (after + before)
                moves.append(after - before)
                edge = pltpu.roll(faces[2, 2 * f + half, pl.ds(b, 8), :], lax.rem(128 - i, 128), 1)
                before = jnp.where(third == 0, edge, pltpu.roll(here, 1, 1))
                edge = pltpu.roll(faces[3, 2 * f + half, pl.ds(b, 8), :], 15 - i, 1)
                after = jnp.where(third == 15, edge, pltpu.roll(here, 127, 1))
                total = total + (after + before)
                moves.append(after - before)
                sums.append(total)
                differences.append(moves)
            for g in range(5):
                flux = None
                for a in range(3):
                    for f in range(5):
                        term = mix_s[a, g, f] * differences[f][a]
                        flux = term if flux is None else flux + term
                value = values[g][half] + (spread * sums[g] - drift * flux)
                out[g, pl.ds(b, 8), pl.ds(pl.multiple_of((2 * i + half) * 128, 128), 128)] = value
        return c

    lax.fori_loop(0, 32, step, 0)
    bytes_of(recv_a.at[pl.ds(0, N - 1)], send_sem.at[0]).wait()
    for at, ref in ((1, send_ar), (2, send_b), (3, send_br)):
        bytes_of(ref.at[pl.ds(0, N - 1)], send_sem.at[at]).wait()
    for at in range(4):
        bytes_of(outbox.at[at], far_send.at[at]).wait()


def shards(old_state, old_map, new_map, box_level, ghost_list, coupling):
    vmem = pl.BlockSpec(memory_space=pltpu.VMEM)
    anywhere = pl.BlockSpec(memory_space=pl.ANY)
    f32, i32 = jnp.float32, jnp.int32
    dma = pltpu.SemaphoreType.DMA
    stepped = pl.pallas_call(
        kernel,
        out_shape=jax.ShapeDtypeStruct((5, BOXES, 4096), f32),
        in_specs=[anywhere] * 7,
        out_specs=vmem,
        scratch_shapes=[
            pltpu.VMEM((BOXES, 4096), f32),
            pltpu.VMEM((N, 4, 128), f32),
            pltpu.VMEM((N, BOXES, 128), f32),
            pltpu.VMEM((N, 4, 128), f32),
            pltpu.VMEM((2048, 128), f32),
            pltpu.VMEM((N, BOXES, 128), f32),
            pltpu.VMEM((N, 4, 128), f32),
            pltpu.VMEM((N, 4, 128), f32),
            pltpu.VMEM((5 * PITCH, BOXES, 128), f32),
            pltpu.VMEM((32, 128), i32),
            pltpu.SMEM((32, 128), i32),
            pltpu.SMEM((2048,), i32),
            pltpu.SMEM((2048,), i32),
            pltpu.SMEM((2048,), i32),
            pltpu.SMEM((6, 4, 2048), i32),
            pltpu.SMEM((3, 5, 5), f32),
            pltpu.VMEM((16, 128), i32),
            pltpu.VMEM((6, 16, 128), i32),
            pltpu.VMEM((16, 128), i32),
            pltpu.VMEM((8, 128), i32),
            pltpu.SMEM((8, 128), i32),
            pltpu.VMEM((49, 10, BOXES, 128), f32),
            pltpu.VMEM((4, 10, ROWS, 128), f32),
            pltpu.VMEM((5, 10, ROWS, 128), f32),
            pltpu.VMEM((10, 96, 128), f32),
            pltpu.VMEM((10, 96, 128), f32),
            pltpu.VMEM((4, 10, BOXES, 128), f32),
            dma((8,)),
            dma((4,)),
            dma((4,)),
            dma((2,)),
            dma((4,)),
            dma((4,)),
        ],
        compiler_params=pltpu.CompilerParams(
            collective_id=0, has_side_effects=True, vmem_limit_bytes=48 << 20),
    )(
        old_state.transpose(1, 0, 2), old_map, new_map, new_map.reshape(16, 128), box_level,
        ghost_list.transpose(1, 2, 0), coupling,
    )
    return stepped.transpose(1, 0, 2)


def solution(mesh):
    return jax.shard_map(
        shards,
        mesh=mesh,
        in_specs=(P("boxes", None, None), P(), P(), P(), P(), P()),
        out_specs=P("boxes", None, None),
        check_vma=False,
    )
```

```python
import jax
import jax.numpy as jnp
from jax import lax
from jax.experimental import pallas as pl
from jax.experimental.pallas import tpu as pltpu
from jax.sharding import PartitionSpec as P

MESH = pl.DeviceIdType.MESH
N = 128
BOXES = 16
STRIDE = 37
DISTANCES = (-2, 2, -1, 1)
ROOM = 20
ROWS = 24
PITCH = 36
BLOCK = 10 * BOXES
diffusion_number = 0.12
advection_number = 0.25


def partner(me, k):
    return lax.rem(me + k * STRIDE, N)


def bytes_of(ref, sem):
    return pltpu.make_async_copy(ref, ref, sem)


def put(src, dst, send_sem, recv_sem, device):
    pltpu.make_async_remote_copy(
        src_ref=src, dst_ref=dst, send_sem=send_sem, recv_sem=recv_sem, device_id=(device,), device_id_type=MESH,
    ).start()


def iota(shape, axis):
    return lax.broadcasted_iota(jnp.int32, shape, axis)


def running_count(chosen):
    lane = iota(chosen.shape, 1)
    count = chosen.astype(jnp.int32)
    for step in (1, 2, 4, 8, 16, 32, 64):
        count = count + jnp.where(lane >= step, pltpu.roll(count, step, 1), 0)
    return count


def swap_bits(rows, unit, steps):
    lane = iota(rows[0].shape, 1)
    rows = list(rows)
    for step in steps:
        high = (lane & (unit * step)) != 0
        for at in range(len(rows)):
            if at & step:
                continue
            low_row, high_row = rows[at], rows[at + step]
            rows[at] = jnp.where(high, pltpu.roll(high_row, unit * step, 1), low_row)
            rows[at + step] = jnp.where(high, high_row, pltpu.roll(low_row, 128 - unit * step, 1))
    return rows


def kernel(state, old_map, new_map, new_lanes, box_level, ghost_list, coupling, out,
           rest, send_ar, recv_a, recv_ar, rolled, send_b, send_br, recv_br, cells, src_v, src_s,
           old_s, new_s, level_s, ghost_s, mix_s, new_v, face_code, level_v, table_v, table_s,
           planes, outbox, inbox, raw, raw_far, faces,
           load_sem, send_sem, recv_sem, small_sem, far_send, far_recv):
    me = lax.axis_index("boxes")
    barrier = pltpu.get_barrier_semaphore()

    def greet(k, c):
        pl.semaphore_signal(barrier, inc=1, device_id=(partner(me, k),), device_id_type=MESH)
        return c

    lax.fori_loop(1, N, greet, 0)
    loads = [
        pltpu.make_async_copy(state.at[4], rest, load_sem.at[0]),
        pltpu.make_async_copy(old_map, old_s, load_sem.at[1]),
        pltpu.make_async_copy(new_map, new_s, load_sem.at[2]),
        pltpu.make_async_copy(new_lanes, new_v, load_sem.at[3]),
        pltpu.make_async_copy(box_level, level_s, load_sem.at[4]),
        pltpu.make_async_copy(ghost_list, ghost_s, load_sem.at[5]),
        pltpu.make_async_copy(coupling, mix_s, load_sem.at[6]),
    ]
    for load in loads:
        load.start()

    def piece(m):
        return state.at[m // 32, :, pl.ds(pl.multiple_of(lax.rem(m, 32) * 128, 128), 128)]

    own = pltpu.make_async_copy(piece(me), recv_a.at[me], load_sem.at[7])
    own.start()
    pl.semaphore_wait(barrier, N - 1)

    def scatter(k, c):
        m = partner(me, k)
        put(piece(m), recv_a.at[me], send_sem.at[0], recv_sem.at[0], m)
        return c

    lax.fori_loop(1, N, scatter, 0)
    loads[0].wait()

    def pack_rest(r, c):
        tile = rest[:, pl.ds(pl.multiple_of(r * 128, 128), 128)]
        for q in range(4):
            send_ar[r * 4 + q] = jnp.concatenate(
                [tile[4 * b:4 * b + 4, 32 * q:32 * q + 32] for b in range(4)], axis=1)
        return c

    lax.fori_loop(0, 32, pack_rest, 0)

    def scatter_rest(k, c):
        m = partner(me, k)
        put(send_ar.at[m], recv_ar.at[me], send_sem.at[1], recv_sem.at[1], m)
        return c

    lax.fori_loop(1, N, scatter_rest, 0)
    recv_ar[me] = send_ar[me]
    for load in loads[1:]:
        load.wait()

    wanted = new_v[...]

    def find(s, c):
        return jnp.where(wanted == old_s[s], s, c)

    source = lax.fori_loop(0, 2048, find, jnp.zeros((16, 128), jnp.int32), unroll=8)
    lane = iota((16, 128), 1)
    turn = (lane // 4 - source // 4 + 8) % 4
    src_v[0:16] = source
    src_v[16:32] = turn * 512 + source // 16 * 4 + source % 4
    to_scalars = pltpu.make_async_copy(src_v, src_s, small_sem.at[0])
    to_scalars.start()

    row8, lane8 = iota((8, 128), 0), iota((8, 128), 1)
    row16 = iota((16, 128), 0)
    nothing = jnp.full((8, 128), -1, jnp.int32)
    zeros16 = jnp.zeros((16, 128), jnp.int32)

    def read_wishes(k, c):
        theirs, their_plane, ours, our_plane, level_here, codes = c
        for at, distance in enumerate(DISTANCES):
            b = new_s[lax.rem(me + distance + N, N) * BOXES + k]
            for f in range(6):
                here = (row8 == at) & (lane8 == f * 16 + k)
                theirs = jnp.where(here, ghost_s[f, 0, b], theirs)
                their_plane = jnp.where(here, ghost_s[f, 1, b], their_plane)
        b = new_s[me * BOXES + k]
        level = level_s[b]
        level_here = jnp.where(row16 == k, level, level_here)
        new_codes = []
        for f in range(6):
            here = lane8 == f * 16 + k
            g = ghost_s[f, 0, b]
            ours = jnp.where(here, g, ours)
            our_plane = jnp.where(here, ghost_s[f, 1, b], our_plane)
            coarser = (level_s[jnp.maximum(g, 0)] < level).astype(jnp.int32)
            code = ghost_s[f, 2, b] // 8 + ghost_s[f, 3, b] // 8 * 2 + coarser * 4
            new_codes.append(jnp.where(row16 == k, code, codes[f]))
        return theirs, their_plane, ours, our_plane, level_here, tuple(new_codes)

    theirs, their_plane, ours, our_plane, level_here, codes = lax.fori_loop(
        0, BOXES, read_wishes, (nothing, nothing, nothing, nothing, zeros16, (zeros16,) * 6))
    level_v[...] = level_here
    for f in range(6):
        face_code[f] = codes[f]

    def find_theirs(t, c):
        return jnp.where(theirs == new_s[me * BOXES + t], t, c)

    their_slot = lax.fori_loop(0, BOXES, find_theirs, nothing)

    def find_ours(t, c):
        return jnp.where(ours == new_s[lax.rem((me - 2 + N) * BOXES + t, N * BOXES)], t, c)

    our_slot = lax.fori_loop(0, 5 * BOXES, find_ours, nothing)
    axis = lane8 // 32
    chosen = their_slot >= 0
    count = running_count(chosen)
    base = (axis * 16 + their_plane) * BLOCK + their_slot
    table = jnp.zeros((8, 128), jnp.int32)
    for j in range(ROOM):
        first = jnp.sum(jnp.where(chosen & (count == j + 1), base, 0), axis=1, keepdims=True)
        table = jnp.where(lane8 == j, first, table)
    low = jnp.where(row8 == 4, 32, 0)
    for at, distance in enumerate(DISTANCES):
        low = jnp.where(row8 == at, 16 * (distance + 2), low)
    chosen = (our_slot >= low) & (our_slot < low + 16) & (row8 < 5)
    count = running_count(chosen)
    far_base = jnp.sum(
        jnp.where(chosen & (row8 < 4), row8 * (10 * ROWS) + count - 1 - 40 * ROWS, 0), axis=0, keepdims=True)
    near_base = jnp.sum(
        jnp.where(chosen & (row8 == 4), (axis * 16 + our_plane) * BLOCK + our_slot - 32 - 48 * BLOCK, 0),
        axis=0, keepdims=True)
    table = jnp.where(row8 == 4, far_base + 40 * ROWS, table)
    table = jnp.where(row8 == 5, near_base + 48 * BLOCK, table)
    table_v[...] = table
    to_table = pltpu.make_async_copy(table_v, table_s, small_sem.at[1])
    to_table.start()
    planes[48] = jnp.zeros((10, BOXES, 128), jnp.float32)
    inbox[4] = jnp.zeros((10, ROWS, 128), jnp.float32)
    for f in range(5):
        for edge in (0, 1, 34, 35):
            cells[f * PITCH + edge] = jnp.zeros((BOXES, 128), jnp.float32)
    to_scalars.wait()
    to_table.wait()

    own.wait()
    bytes_of(recv_a.at[pl.ds(0, N - 1)], recv_sem.at[0]).wait()
    arrived = recv_a.reshape(2048, 128)
    landing = me // 32 * PITCH + 2 + lax.rem(me, 32)

    def gather(d, into):
        hi = d // 8
        lo = lax.rem(d, 8) * 16
        for t in range(16):
            into[pl.ds(t, 1), :] = arrived[pl.ds(src_s[hi, lo + t], 1), :]

    def forward(k, c):
        d = partner(me, k)
        gather(d, send_b.at[d])
        put(send_b.at[d], cells.at[landing], send_sem.at[2], recv_sem.at[2], d)
        return c

    lax.fori_loop(1, N, forward, 0)
    gather(me, cells.at[landing])
    bytes_of(recv_ar.at[pl.ds(0, N - 1)], recv_sem.at[1]).wait()

    def turn_rest(s, c):
        part = recv_ar[pl.ds(s * 4, 4)].reshape(16, 128)
        for t in range(4):
            rolled[pl.ds(pl.multiple_of(t * 512 + s * 16, 16), 16), :] = (
                pltpu.roll(part, 32 * t, 1) if t else part)
        return c

    lax.fori_loop(0, 32, turn_rest, 0)
    lane1 = iota((1, 128), 1)

    def gather_rest(d, into):
        hi = 16 + d // 8
        lo = lax.rem(d, 8) * 16
        for q in range(4):
            part = [rolled[pl.ds(src_s[hi, lo + i * 4 + q], 1), :] for i in range(4)]
            into[pl.ds(q, 1), :] = jnp.where(
                lane1 < 64, jnp.where(lane1 < 32, part[0], part[1]), jnp.where(lane1 < 96, part[2], part[3]))

    def forward_rest(k, c):
        d = partner(me, k)
        gather_rest(d, send_br.at[d])
        put(send_br.at[d], recv_br.at[me], send_sem.at[3], recv_sem.at[3], d)
        return c

    lax.fori_loop(1, N, forward_rest, 0)
    gather_rest(me, recv_br.at[me])
    bytes_of(cells.at[pl.ds(0, N - 1)], recv_sem.at[2]).wait()

    def transpose_planes(at, c):
        f, half, b = at >> 2, (at >> 1) & 1, pl.multiple_of((at & 1) * 8, 8)
        rows = [cells[f * PITCH + 2 + 2 * i + half, pl.ds(b, 8), :] for i in range(16)]
        for i in range(16):
            planes[i, 2 * f + half, pl.ds(b, 8), :] = rows[i]
        for upper in range(2):
            turned = swap_bits(rows[8 * upper:8 * upper + 8], 16, (4, 2, 1))
            for j in range(8):
                planes[16 + 8 * half + j, 2 * f + upper, pl.ds(b, 8), :] = turned[j]
        turned = swap_bits(rows, 1, (8, 4, 2, 1))
        for k in range(16):
            planes[32 + k, 2 * f + half, pl.ds(b, 8), :] = turned[k]
        return c

    lax.fori_loop(0, 16, transpose_planes, 0)
    bytes_of(recv_br.at[pl.ds(0, N - 1)], recv_sem.at[3]).wait()

    def unpack_rest(r, c):
        parts = [recv_br[pl.ds(r * 32 + q, 8, stride=4)].reshape(32, 128) for q in range(4)]
        for b, part in enumerate(swap_bits(parts, 32, (2, 1))):
            cells[pl.ds(4 * PITCH + 2 + 8 * r, 8), 4 * b:4 * b + 4, :] = part.reshape(8, 4, 128)
        return c

    lax.fori_loop(0, 4, unpack_rest, 0)
    lax.fori_loop(16, 20, transpose_planes, 0)
    plane_rows = planes.reshape(49 * BLOCK, 128)

    for at, distance in enumerate(DISTANCES):
        def fill(j, c, at=at):
            base = table_s[at, j]
            for h in range(10):
                outbox[at, h, pl.ds(j, 1), :] = plane_rows[pl.ds(base + h * BOXES, 1), :]
            return c

        lax.fori_loop(0, ROOM, fill, 0, unroll=4)
        put(outbox.at[at], inbox.at[at ^ 1], far_send.at[at], far_recv.at[at ^ 1],
            lax.rem(me + distance + N, N))

    def take_near(q, c):
        base = table_s[5, q]
        for h in range(10):
            raw[h, pl.ds(q, 1), :] = plane_rows[pl.ds(base + h * BOXES, 1), :]
        return c

    lax.fori_loop(0, 96, take_near, 0, unroll=4)

    lane = iota((8, 128), 1)
    third = lane & 15

    def factors(b):
        scale = (2 - level_v[pl.ds(b, 8), :]).astype(jnp.float32)
        return diffusion_number / (scale * scale), advection_number / scale * 0.5

    def step(at, c):
        i, b = at >> 1, pl.multiple_of((at & 1) * 8, 8)
        spread, drift = factors(b)

        def at_row(f, r):
            return cells[f * PITCH + 2 + r, pl.ds(b, 8), :]

        values = [[at_row(f, 2 * i + h) for h in range(2)] for f in range(5)]
        for half in range(2):
            sums, differences = [], []
            for f in range(5):
                here, other = values[f][half], values[f][1 - half]
                before, after = at_row(f, 2 * i + half - 2), at_row(f, 2 * i + half + 2)
                total = after + before - 6.0 * here
                moves = [after - before]
                if half == 0:
                    before = jnp.where(lane < 16, 0.0, pltpu.roll(here, 16, 1))
                    after = pltpu.roll(jnp.where(lane < 16, other, here), 112, 1)
                else:
                    before = pltpu.roll(jnp.where(lane >= 112, other, here), 16, 1)
                    after = jnp.where(lane >= 112, 0.0, pltpu.roll(here, 112, 1))
                total = total + (after + before)
                moves.append(after - before)
                before = jnp.where(third == 0, 0.0, pltpu.roll(here, 1, 1))
                after = jnp.where(third == 15, 0.0, pltpu.roll(here, 127, 1))
                total = total + (after + before)
                moves.append(after - before)
                sums.append(total)
                differences.append(moves)
            for g in range(5):
                flux = None
                for a in range(3):
                    for f in range(5):
                        term = mix_s[g, a, f] * differences[f][a]
                        flux = term if flux is None else flux + term
                value = values[g][half] + (spread * sums[g] - drift * flux)
                out[g, pl.ds(b, 8), pl.ds(pl.multiple_of((2 * i + half) * 128, 128), 128)] = value
        return c

    lax.fori_loop(0, 32, step, 0)

    for at in range(4):
        bytes_of(inbox.at[at], far_recv.at[at]).wait()
    inbox_rows = inbox.reshape(50 * ROWS, 128)

    def take_far(q, c):
        base = table_s[4, q]
        for h in range(10):
            raw_far[h, pl.ds(q, 1), :] = inbox_rows[pl.ds(base + h * ROWS, 1), :]
        return c

    lax.fori_loop(0, 96, take_far, 0, unroll=4)

    for face in range(6):
        def add_face(part, c, face=face):
            b = pl.multiple_of(part * 8, 8)
            spread, drift = factors(b)
            code = face_code[face, pl.ds(b, 8), :]
            coarse = code >= 4
            first, second = code & 1, (code >> 1) & 1
            if face >= 4:
                first, second = second, first
            low_first = coarse & (first == 0)
            high_first = coarse & (first == 1)
            fine_pick = ((lane >> 5) << 4) + second * 8 + ((lane & 15) >> 1)
            picks = [jnp.where(coarse, 64 * half + fine_pick, lane) for half in range(2)]
            ghost = []
            for f in range(5):
                rows = pl.ds(16 * face + b, 8)
                half = [raw[2 * f + h, rows, :] + raw_far[2 * f + h, rows, :] for h in range(2)]
                chosen = [jnp.where(high_first, half[1], half[0]), jnp.where(low_first, half[0], half[1])]
                ghost.append([
                    jnp.take_along_axis(chosen[h], picks[h], axis=1, mode="promise_in_bounds")
                    for h in range(2)])
            for g in range(5):
                for h in range(2):
                    flux = None
                    for f in range(5):
                        term = mix_s[g, face // 2, f] * ghost[f][h]
                        flux = term if flux is None else flux + term
                    sign = drift if face % 2 == 0 else -drift
                    value = spread * ghost[g][h] + sign * flux
                    if face < 2:
                        at = (30 * face + h) * 128
                        out[g, pl.ds(b, 8), at:at + 128] = out[g, pl.ds(b, 8), at:at + 128] + value
                    else:
                        faces[face - 2, 2 * g + h, pl.ds(b, 8), :] = value
            return c

        lax.fori_loop(0, 2, add_face, 0)

    def spread_faces(at, c):
        i, b = at >> 1, pl.multiple_of((at & 1) * 8, 8)
        eighth = (i & 7) * 16
        upper = i >> 3
        for g in range(5):
            for half in range(2):
                cut = pl.ds(pl.multiple_of((2 * i + half) * 128, 128), 128)
                lower_third = pltpu.roll(faces[2, 2 * g + half, pl.ds(b, 8), :], (128 - i) & 127, 1)
                upper_third = pltpu.roll(faces[3, 2 * g + half, pl.ds(b, 8), :], 15 - i, 1)
                value = out[g, pl.ds(b, 8), cut] + jnp.where(
                    third == 0, lower_third, jnp.where(third == 15, upper_third, 0.0))
                if half == 0:
                    edge = pltpu.roll(faces[0, 2 * g + upper, pl.ds(b, 8), :], (128 - eighth) & 127, 1)
                    value = value + jnp.where(lane < 16, edge, 0.0)
                else:
                    edge = pltpu.roll(faces[1, 2 * g + upper, pl.ds(b, 8), :], 112 - eighth, 1)
                    value = value + jnp.where(lane >= 112, edge, 0.0)
                out[g, pl.ds(b, 8), cut] = value
        return c

    lax.fori_loop(0, 32, spread_faces, 0)
    bytes_of(recv_a.at[pl.ds(0, N - 1)], send_sem.at[0]).wait()
    for at, ref in ((1, send_ar), (2, send_b), (3, send_br)):
        bytes_of(ref.at[pl.ds(0, N - 1)], send_sem.at[at]).wait()
    for at in range(4):
        bytes_of(outbox.at[at], far_send.at[at]).wait()


def shards(old_state, old_map, new_map, box_level, ghost_list, coupling):
    vmem = pl.BlockSpec(memory_space=pltpu.VMEM)
    hbm = pl.BlockSpec(memory_space=pltpu.HBM)
    f32, i32 = jnp.float32, jnp.int32
    dma = pltpu.SemaphoreType.DMA
    stepped = pl.pallas_call(
        kernel,
        out_shape=jax.ShapeDtypeStruct((5, BOXES, 4096), f32),
        in_specs=[hbm] * 7,
        out_specs=vmem,
        scratch_shapes=[
            pltpu.VMEM((BOXES, 4096), f32),
            pltpu.VMEM((N, 4, 128), f32),
            pltpu.VMEM((N, BOXES, 128), f32),
            pltpu.VMEM((N, 4, 128), f32),
            pltpu.VMEM((2048, 128), f32),
            pltpu.VMEM((N, BOXES, 128), f32),
            pltpu.VMEM((N, 4, 128), f32),
            pltpu.VMEM((N, 4, 128), f32),
            pltpu.VMEM((5 * PITCH, BOXES, 128), f32),
            pltpu.VMEM((32, 128), i32),
            pltpu.SMEM((32, 128), i32),
            pltpu.SMEM((2048,), i32),
            pltpu.SMEM((2048,), i32),
            pltpu.SMEM((2048,), i32),
            pltpu.SMEM((6, 4, 2048), i32),
            pltpu.SMEM((5, 3, 5), f32),
            pltpu.VMEM((16, 128), i32),
            pltpu.VMEM((6, 16, 128), i32),
            pltpu.VMEM((16, 128), i32),
            pltpu.VMEM((8, 128), i32),
            pltpu.SMEM((8, 128), i32),
            pltpu.VMEM((49, 10, BOXES, 128), f32),
            pltpu.VMEM((4, 10, ROWS, 128), f32),
            pltpu.VMEM((5, 10, ROWS, 128), f32),
            pltpu.VMEM((10, 96, 128), f32),
            pltpu.VMEM((10, 96, 128), f32),
            pltpu.VMEM((4, 10, BOXES, 128), f32),
            dma((8,)),
            dma((4,)),
            dma((4,)),
            dma((2,)),
            dma((4,)),
            dma((4,)),
        ],
        compiler_params=pltpu.CompilerParams(
            collective_id=0, has_side_effects=True, vmem_limit_bytes=48 << 20),
    )(
        old_state.transpose(1, 0, 2), old_map, new_map, new_map.reshape(16, 128), box_level,
        ghost_list.transpose(1, 2, 0), coupling.transpose(1, 0, 2),
    )
    return stepped.transpose(1, 0, 2)


def solution(mesh):
    return jax.shard_map(
        shards,
        mesh=mesh,
        in_specs=(P("boxes", None, None), P(), P(), P(), P(), P()),
        out_specs=P("boxes", None, None),
        check_vma=False,
    )
```

```python
import jax
import jax.numpy as jnp
from jax import lax
from jax.experimental import pallas as pl
from jax.experimental.pallas import tpu as pltpu
from jax.sharding import PartitionSpec as P

MESH = pl.DeviceIdType.MESH
N = 128
BOXES = 16
STRIDE = 27
DISTANCES = (-2, 2, -1, 1)
ROOM = 20
ROWS = 24
PITCH = 36
BLOCK = 10 * BOXES
EARLY = 24
diffusion_number = 0.12
advection_number = 0.25


def partner(me, k):
    return lax.rem(me + k * STRIDE, N)


def bytes_of(ref, sem):
    return pltpu.make_async_copy(ref, ref, sem)


def put(src, dst, send_sem, recv_sem, device):
    pltpu.make_async_remote_copy(
        src_ref=src, dst_ref=dst, send_sem=send_sem, recv_sem=recv_sem, device_id=(device,), device_id_type=MESH,
    ).start()


def iota(shape, axis):
    return lax.broadcasted_iota(jnp.int32, shape, axis)


def running_count(chosen):
    lane = iota(chosen.shape, 1)
    count = chosen.astype(jnp.int32)
    for step in (1, 2, 4, 8, 16, 32, 64):
        count = count + jnp.where(lane >= step, pltpu.roll(count, step, 1), 0)
    return count


def swap_bits(rows, unit, steps):
    lane = iota(rows[0].shape, 1)
    rows = list(rows)
    for step in steps:
        high = (lane & (unit * step)) != 0
        for at in range(len(rows)):
            if at & step:
                continue
            low_row, high_row = rows[at], rows[at + step]
            crossed = jnp.where(high, low_row, high_row)
            if unit * step == 64:
                crossed = pltpu.roll(crossed, 64, 1)
            else:
                crossed = jnp.take_along_axis(crossed, lane ^ (unit * step), axis=1, mode="promise_in_bounds")
            rows[at] = jnp.where(high, crossed, low_row)
            rows[at + step] = jnp.where(high, high_row, crossed)
    return rows


def kernel(state, old_map, new_map, new_lanes, box_level, ghost_list, coupling, out,
           rest, send_ar, recv_a, recv_ar, rolled, send_b, send_br, recv_br, cells, src_v, src_s,
           old_s, new_s, level_s, ghost_s, mix_s, new_v, face_code, level_v, table_v, table_s,
           planes, outbox, inbox, inbox_last, raw, raw_far, faces,
           load_sem, send_sem, recv_sem, small_sem, far_send, far_recv):
    me = lax.axis_index("boxes")
    barrier = pltpu.get_barrier_semaphore()

    def greet(k, c):
        pl.semaphore_signal(barrier, inc=1, device_id=(partner(me, k),), device_id_type=MESH)
        return c

    lax.fori_loop(1, N, greet, 0)
    loads = [
        pltpu.make_async_copy(state.at[4], rest, load_sem.at[0]),
        pltpu.make_async_copy(old_map, old_s, load_sem.at[1]),
        pltpu.make_async_copy(new_map, new_s, load_sem.at[2]),
        pltpu.make_async_copy(new_lanes, new_v, load_sem.at[3]),
        pltpu.make_async_copy(box_level, level_s, load_sem.at[4]),
        pltpu.make_async_copy(ghost_list, ghost_s, load_sem.at[5]),
        pltpu.make_async_copy(coupling, mix_s, load_sem.at[6]),
    ]
    for load in loads:
        load.start()

    def piece(m):
        return state.at[m // 32, :, pl.ds(pl.multiple_of(lax.rem(m, 32) * 128, 128), 128)]

    own = pltpu.make_async_copy(piece(me), recv_a.at[me], load_sem.at[7])
    own.start()
    pl.semaphore_wait(barrier, N - 1)

    def scatter(k, c):
        m = partner(me, k)
        put(piece(m), recv_a.at[me], send_sem.at[0], recv_sem.at[0], m)
        return c

    lax.fori_loop(1, N, scatter, 0)
    loads[0].wait()

    def pack_rest(r, c):
        tile = rest[:, pl.ds(pl.multiple_of(r * 128, 128), 128)]
        for q in range(4):
            send_ar[r * 4 + q] = jnp.concatenate(
                [tile[4 * b:4 * b + 4, 32 * q:32 * q + 32] for b in range(4)], axis=1)
        return c

    lax.fori_loop(0, 32, pack_rest, 0)

    def scatter_rest(k, c):
        m = partner(me, k)
        put(send_ar.at[m], recv_ar.at[me], send_sem.at[1], recv_sem.at[1], m)
        return c

    lax.fori_loop(1, N, scatter_rest, 0)
    recv_ar[me] = send_ar[me]
    for load in loads[1:]:
        load.wait()

    wanted = new_v[...]

    def find(s, c):
        return jnp.where(wanted == old_s[s], s, c)

    source = lax.fori_loop(0, 2048, find, jnp.zeros((16, 128), jnp.int32), unroll=8)
    lane = iota((16, 128), 1)
    turn = (lane // 4 - source // 4 + 8) % 4
    src_v[0:16] = source
    src_v[16:32] = turn * 512 + source // 16 * 4 + source % 4
    to_scalars = pltpu.make_async_copy(src_v, src_s, small_sem.at[0])
    to_scalars.start()

    row8, lane8 = iota((8, 128), 0), iota((8, 128), 1)
    row16 = iota((16, 128), 0)
    nothing = jnp.full((8, 128), -1, jnp.int32)
    zeros16 = jnp.zeros((16, 128), jnp.int32)

    def read_wishes(k, c):
        theirs, their_plane, ours, our_plane, level_here, codes = c
        for at, distance in enumerate(DISTANCES):
            b = new_s[lax.rem(me + distance + N, N) * BOXES + k]
            for f in range(6):
                here = (row8 == at) & (lane8 == f * 16 + k)
                theirs = jnp.where(here, ghost_s[f, 0, b], theirs)
                their_plane = jnp.where(here, ghost_s[f, 1, b], their_plane)
        b = new_s[me * BOXES + k]
        level = level_s[b]
        level_here = jnp.where(row16 == k, level, level_here)
        new_codes = []
        for f in range(6):
            here = lane8 == f * 16 + k
            g = ghost_s[f, 0, b]
            ours = jnp.where(here, g, ours)
            our_plane = jnp.where(here, ghost_s[f, 1, b], our_plane)
            coarser = (level_s[jnp.maximum(g, 0)] < level).astype(jnp.int32)
            code = ghost_s[f, 2, b] // 8 + ghost_s[f, 3, b] // 8 * 2 + coarser * 4
            new_codes.append(jnp.where(row16 == k, code, codes[f]))
        return theirs, their_plane, ours, our_plane, level_here, tuple(new_codes)

    theirs, their_plane, ours, our_plane, level_here, codes = lax.fori_loop(
        0, BOXES, read_wishes, (nothing, nothing, nothing, nothing, zeros16, (zeros16,) * 6))
    level_v[...] = level_here
    for f in range(6):
        face_code[f] = codes[f]

    def find_theirs(t, c):
        return jnp.where(theirs == new_s[me * BOXES + t], t, c)

    their_slot = lax.fori_loop(0, BOXES, find_theirs, nothing)

    def find_ours(t, c):
        return jnp.where(ours == new_s[lax.rem((me - 2 + N) * BOXES + t, N * BOXES)], t, c)

    our_slot = lax.fori_loop(0, 5 * BOXES, find_ours, nothing)
    axis = lane8 // 32
    chosen = their_slot >= 0
    count = running_count(chosen)
    base = (axis * 16 + their_plane) * BLOCK + their_slot
    table = jnp.zeros((8, 128), jnp.int32)
    for j in range(ROOM):
        first = jnp.sum(jnp.where(chosen & (count == j + 1), base, 0), axis=1, keepdims=True)
        table = jnp.where(lane8 == j, first, table)
    low = jnp.where(row8 == 4, 32, 0)
    for at, distance in enumerate(DISTANCES):
        low = jnp.where(row8 == at, 16 * (distance + 2), low)
    chosen = (our_slot >= low) & (our_slot < low + 16) & (row8 < 5)
    count = running_count(chosen)
    for row, count_of in ((4, 8), (6, 2)):
        pitch = count_of * ROWS
        far_base = jnp.sum(
            jnp.where(chosen & (row8 < 4), row8 * pitch + count - 1 - 4 * pitch, 0), axis=0, keepdims=True)
        table = jnp.where(row8 == row, far_base + 4 * pitch, table)
    near_base = jnp.sum(
        jnp.where(chosen & (row8 == 4), (axis * 16 + our_plane) * BLOCK + our_slot - 32 - 48 * BLOCK, 0),
        axis=0, keepdims=True)
    table = jnp.where(row8 == 5, near_base + 48 * BLOCK, table)
    table_v[...] = table
    to_table = pltpu.make_async_copy(table_v, table_s, small_sem.at[1])
    to_table.start()
    planes[48] = jnp.zeros((10, BOXES, 128), jnp.float32)
    inbox[4] = jnp.zeros((8, ROWS, 128), jnp.float32)
    inbox_last[4] = jnp.zeros((2, ROWS, 128), jnp.float32)
    for f in range(5):
        for edge in (0, 1, 34, 35):
            cells[f * PITCH + edge] = jnp.zeros((BOXES, 128), jnp.float32)
    to_scalars.wait()
    to_table.wait()

    own.wait()
    bytes_of(recv_a.at[pl.ds(0, N - 1)], recv_sem.at[0]).wait()
    arrived = recv_a.reshape(2048, 128)
    landing = me // 32 * PITCH + 2 + lax.rem(me, 32)

    def gather(d, into):
        hi = d // 8
        lo = lax.rem(d, 8) * 16
        for t in range(16):
            into[pl.ds(t, 1), :] = arrived[pl.ds(src_s[hi, lo + t], 1), :]

    def forward(k, c):
        d = partner(me, k)
        gather(d, send_b.at[d])
        put(send_b.at[d], cells.at[landing], send_sem.at[2], recv_sem.at[2], d)
        return c

    lax.fori_loop(1, N, forward, 0)
    gather(me, cells.at[landing])
    bytes_of(recv_ar.at[pl.ds(0, N - 1)], recv_sem.at[1]).wait()

    def turn_rest(s, c):
        part = recv_ar[pl.ds(s * 4, 4)].reshape(16, 128)
        for t in range(4):
            rolled[pl.ds(pl.multiple_of(t * 512 + s * 16, 16), 16), :] = (
                pltpu.roll(part, 32 * t, 1) if t else part)
        return c

    lax.fori_loop(0, 32, turn_rest, 0)
    lane1 = iota((1, 128), 1)

    def gather_rest(d, into):
        hi = 16 + d // 8
        lo = lax.rem(d, 8) * 16
        for q in range(4):
            part = [rolled[pl.ds(src_s[hi, lo + i * 4 + q], 1), :] for i in range(4)]
            into[pl.ds(q, 1), :] = jnp.where(
                lane1 < 64, jnp.where(lane1 < 32, part[0], part[1]), jnp.where(lane1 < 96, part[2], part[3]))

    def forward_rest(k, c):
        d = partner(me, k)
        gather_rest(d, send_br.at[d])
        put(send_br.at[d], recv_br.at[me], send_sem.at[3], recv_sem.at[3], d)
        return c

    lax.fori_loop(1, N, forward_rest, 0)
    gather_rest(me, recv_br.at[me])
    bytes_of(cells.at[pl.ds(0, N - 1)], recv_sem.at[2]).wait()

    def transpose_planes(at, c):
        f, half, b = at >> 2, (at >> 1) & 1, pl.multiple_of((at & 1) * 8, 8)
        rows = [cells[f * PITCH + 2 + 2 * i + half, pl.ds(b, 8), :] for i in range(16)]
        for i in range(16):
            planes[i, 2 * f + half, pl.ds(b, 8), :] = rows[i]
        for upper in range(2):
            turned = swap_bits(rows[8 * upper:8 * upper + 8], 16, (4, 2, 1))
            for j in range(8):
                planes[16 + 8 * half + j, 2 * f + upper, pl.ds(b, 8), :] = turned[j]
        turned = swap_bits(rows, 1, (8, 4, 2, 1))
        for k in range(16):
            planes[32 + k, 2 * f + half, pl.ds(b, 8), :] = turned[k]
        return c

    plane_rows = planes.reshape(49 * BLOCK, 128)

    def send_planes(first, count, part):
        cut = pl.ds(first, count)
        for at, distance in enumerate(DISTANCES):
            def fill(j, c, at=at):
                base = table_s[at, j]
                for h in range(first, first + count):
                    outbox[at, h, pl.ds(j, 1), :] = plane_rows[pl.ds(base + h * BOXES, 1), :]
                return c

            lax.fori_loop(0, ROOM, fill, 0, unroll=4)
            put(outbox.at[at, cut], (inbox, inbox_last)[part].at[at ^ 1], far_send.at[part, at], far_recv.at[part, at ^ 1],
                lax.rem(me + distance + N, N))

    def take_near(first, count):
        def take(q, c):
            base = table_s[5, q]
            for h in range(first, first + count):
                raw[h, pl.ds(q, 1), :] = plane_rows[pl.ds(base + h * BOXES, 1), :]
            return c

        lax.fori_loop(0, 96, take, 0, unroll=4)

    lane = iota((8, 128), 1)
    third = lane & 15

    def factors(b):
        scale = (2 - level_v[pl.ds(b, 8), :]).astype(jnp.float32)
        return diffusion_number / (scale * scale), advection_number / scale * 0.5

    def step(at, fields):
        i, b = at >> 1, pl.multiple_of((at & 1) * 8, 8)
        spread, drift = factors(b)

        def at_row(f, r):
            return cells[f * PITCH + 2 + r, pl.ds(b, 8), :]

        values = {f: [at_row(f, 2 * i + h) for h in range(2)] for f in fields}
        for half in range(2):
            sums, differences = {}, {}
            for f in fields:
                here, other = values[f][half], values[f][1 - half]
                before, after = at_row(f, 2 * i + half - 2), at_row(f, 2 * i + half + 2)
                total = after + before - 6.0 * here
                moves = [after - before]
                if half == 0:
                    before = jnp.where(lane < 16, 0.0, pltpu.roll(here, 16, 1))
                    after = pltpu.roll(jnp.where(lane < 16, other, here), 112, 1)
                else:
                    before = pltpu.roll(jnp.where(lane >= 112, other, here), 16, 1)
                    after = jnp.where(lane >= 112, 0.0, pltpu.roll(here, 112, 1))
                total = total + (after + before)
                moves.append(after - before)
                before = jnp.where(third == 0, 0.0, pltpu.roll(here, 1, 1))
                after = jnp.where(third == 15, 0.0, pltpu.roll(here, 127, 1))
                total = total + (after + before)
                moves.append(after - before)
                sums[f] = total
                differences[f] = [drift * move for move in moves]
            for g in range(5):
                value = None
                if 0 not in fields:
                    value = out[g, pl.ds(b, 8), pl.ds(pl.multiple_of((2 * i + half) * 128, 128), 128)]
                if g in fields:
                    own = values[g][half] + spread * sums[g]
                    value = own if value is None else value + own
                for a in range(3):
                    for f in fields:
                        term = mix_s[g, a, f] * differences[f][a]
                        value = -term if value is None else value - term
                out[g, pl.ds(b, 8), pl.ds(pl.multiple_of((2 * i + half) * 128, 128), 128)] = value

    def step_four(at, c):
        step(at, (0, 1, 2, 3))
        return c

    def step_last(at, c):
        step(at, (4,))
        return c

    lax.fori_loop(0, 16, transpose_planes, 0, unroll=2)
    send_planes(0, 8, 0)
    lax.fori_loop(0, EARLY, step_four, 0, unroll=2)

    bytes_of(recv_br.at[pl.ds(0, N - 1)], recv_sem.at[3]).wait()

    def unpack_rest(r, c):
        parts = [recv_br[pl.ds(r * 32 + q, 8, stride=4)].reshape(32, 128) for q in range(4)]
        for b, part in enumerate(swap_bits(parts, 32, (2, 1))):
            cells[pl.ds(4 * PITCH + 2 + 8 * r, 8), 4 * b:4 * b + 4, :] = part.reshape(8, 4, 128)
        return c

    lax.fori_loop(0, 4, unpack_rest, 0)
    lax.fori_loop(16, 20, transpose_planes, 0, unroll=2)
    send_planes(8, 2, 1)
    take_near(0, 8)
    take_near(8, 2)
    lax.fori_loop(EARLY, 32, step_four, 0, unroll=2)
    lax.fori_loop(0, 32, step_last, 0, unroll=4)

    def add_face(face, part, fields):
        b = pl.multiple_of(part * 8, 8)
        spread, drift = factors(b)
        code = face_code[face, pl.ds(b, 8), :]
        coarse = code >= 4
        first, second = code & 1, (code >> 1) & 1
        if face >= 4:
            first, second = second, first
        low_first = coarse & (first == 0)
        high_first = coarse & (first == 1)
        fine_pick = ((lane >> 5) << 4) + second * 8 + ((lane & 15) >> 1)
        picks = [jnp.where(coarse, 64 * half + fine_pick, lane) for half in range(2)]
        sign = drift if face % 2 == 0 else -drift
        ghost = {}
        for f in fields:
            rows = pl.ds(16 * face + b, 8)
            half = [raw[2 * f + h, rows, :] + raw_far[2 * f + h, rows, :] for h in range(2)]
            chosen = [jnp.where(high_first, half[1], half[0]), jnp.where(low_first, half[0], half[1])]
            ghost[f] = [
                jnp.take_along_axis(chosen[h], picks[h], axis=1, mode="promise_in_bounds") for h in range(2)]
        for g in range(5):
            for h in range(2):
                flux = None
                for f in fields:
                    term = mix_s[g, face // 2, f] * ghost[f][h]
                    flux = term if flux is None else flux + term
                value = sign * flux
                if g in fields:
                    value = value + spread * ghost[g][h]
                if face < 2:
                    at = (30 * face + h) * 128
                    out[g, pl.ds(b, 8), at:at + 128] = out[g, pl.ds(b, 8), at:at + 128] + value
                elif 0 in fields:
                    faces[face - 2, 2 * g + h, pl.ds(b, 8), :] = value
                else:
                    faces[face - 2, 2 * g + h, pl.ds(b, 8), :] = (
                        faces[face - 2, 2 * g + h, pl.ds(b, 8), :] + value)

    def add_planes(first, count, part, fields):
        landed = (inbox, inbox_last)[part]
        for at in range(4):
            bytes_of(landed.at[at], far_recv.at[part, at]).wait()
        landed_rows = landed.reshape(5 * count * ROWS, 128)

        def take(q, c):
            base = table_s[4 + 2 * part, q]
            for h in range(count):
                raw_far[first + h, pl.ds(q, 1), :] = landed_rows[pl.ds(base + h * ROWS, 1), :]
            return c

        lax.fori_loop(0, 96, take, 0, unroll=4)
        for face in range(6):
            def add(part, c, face=face):
                add_face(face, part, fields)
                return c

            lax.fori_loop(0, 2, add, 0, unroll=2)

    add_planes(0, 8, 0, (0, 1, 2, 3))
    add_planes(8, 2, 1, (4,))

    def spread_faces(at, c):
        g, b = at >> 1, pl.multiple_of((at & 1) * 8, 8)
        halves = [[faces[f, 2 * g + h, pl.ds(b, 8), :] for h in range(2)] for f in range(4)]
        after_second = [pltpu.roll(v, 112, 1) for v in halves[1]]
        after_third = [pltpu.roll(v, 15, 1) for v in halves[3]]
        for i in range(16):
            both = jnp.where(lane >> 4 == i % 8, halves[0][i // 8], after_second[i // 8])
            edge = pltpu.roll(both, (128 - 16 * (i % 8)) % 128, 1) if i % 8 else both
            edges = (jnp.where(lane < 16, edge, 0.0), jnp.where(lane >= 112, edge, 0.0))
            for half in range(2):
                cut = slice((2 * i + half) * 128, (2 * i + half + 1) * 128)
                both = jnp.where(third == i, halves[2][half], after_third[half])
                both = pltpu.roll(both, 128 - i, 1) if i else both
                value = jnp.where((third == 0) | (third == 15), both, 0.0)
                out[g, pl.ds(b, 8), cut] = out[g, pl.ds(b, 8), cut] + (value + edges[half])
        return c

    lax.fori_loop(0, 10, spread_faces, 0, unroll=2)
    bytes_of(recv_a.at[pl.ds(0, N - 1)], send_sem.at[0]).wait()
    for at, ref in ((1, send_ar), (2, send_b), (3, send_br)):
        bytes_of(ref.at[pl.ds(0, N - 1)], send_sem.at[at]).wait()
    for part, cut in enumerate((pl.ds(0, 8), pl.ds(8, 2))):
        for at in range(4):
            bytes_of(outbox.at[at, cut], far_send.at[part, at]).wait()


def shards(old_state, old_map, new_map, box_level, ghost_list, coupling):
    vmem = pl.BlockSpec(memory_space=pltpu.VMEM)
    hbm = pl.BlockSpec(memory_space=pltpu.HBM)
    f32, i32 = jnp.float32, jnp.int32
    dma = pltpu.SemaphoreType.DMA
    stepped = pl.pallas_call(
        kernel,
        out_shape=jax.ShapeDtypeStruct((5, BOXES, 4096), f32),
        in_specs=[hbm] * 7,
        out_specs=vmem,
        scratch_shapes=[
            pltpu.VMEM((BOXES, 4096), f32),
            pltpu.VMEM((N, 4, 128), f32),
            pltpu.VMEM((N, BOXES, 128), f32),
            pltpu.VMEM((N, 4, 128), f32),
            pltpu.VMEM((2048, 128), f32),
            pltpu.VMEM((N, BOXES, 128), f32),
            pltpu.VMEM((N, 4, 128), f32),
            pltpu.VMEM((N, 4, 128), f32),
            pltpu.VMEM((5 * PITCH, BOXES, 128), f32),
            pltpu.VMEM((32, 128), i32),
            pltpu.SMEM((32, 128), i32),
            pltpu.SMEM((2048,), i32),
            pltpu.SMEM((2048,), i32),
            pltpu.SMEM((2048,), i32),
            pltpu.SMEM((6, 4, 2048), i32),
            pltpu.SMEM((5, 3, 5), f32),
            pltpu.VMEM((16, 128), i32),
            pltpu.VMEM((6, 16, 128), i32),
            pltpu.VMEM((16, 128), i32),
            pltpu.VMEM((8, 128), i32),
            pltpu.SMEM((8, 128), i32),
            pltpu.VMEM((49, 10, BOXES, 128), f32),
            pltpu.VMEM((4, 10, ROWS, 128), f32),
            pltpu.VMEM((5, 8, ROWS, 128), f32),
            pltpu.VMEM((5, 2, ROWS, 128), f32),
            pltpu.VMEM((10, 96, 128), f32),
            pltpu.VMEM((10, 96, 128), f32),
            pltpu.VMEM((4, 10, BOXES, 128), f32),
            dma((8,)),
            dma((4,)),
            dma((4,)),
            dma((2,)),
            dma((2, 4)),
            dma((2, 4)),
        ],
        compiler_params=pltpu.CompilerParams(
            collective_id=0, has_side_effects=True, vmem_limit_bytes=48 << 20),
    )(
        old_state.transpose(1, 0, 2), old_map, new_map, new_map.reshape(16, 128), box_level,
        ghost_list.transpose(1, 2, 0), coupling.transpose(1, 0, 2),
    )
    return stepped.transpose(1, 0, 2)


def solution(mesh):
    return jax.shard_map(
        shards,
        mesh=mesh,
        in_specs=(P("boxes", None, None), P(), P(), P(), P(), P()),
        out_specs=P("boxes", None, None),
        check_vma=False,
    )
```

```python
import jax
import jax.numpy as jnp
from jax import lax
from jax.experimental import pallas as pl
from jax.experimental.pallas import tpu as pltpu
from jax.sharding import PartitionSpec as P

MESH = pl.DeviceIdType.MESH
N = 128
BOXES = 16
STRIDE = 27
DISTANCES = (-2, 2, -1, 1)
ROOM = 20
ROWS = 24
PITCH = 36
BLOCK = 10 * BOXES
EARLY = 12
diffusion_number = 0.12
advection_number = 0.25


def partner(me, k):
    return lax.rem(me + k * STRIDE, N)


def bytes_of(ref, sem):
    return pltpu.make_async_copy(ref, ref, sem)


def put(src, dst, send_sem, recv_sem, device):
    pltpu.make_async_remote_copy(
        src_ref=src, dst_ref=dst, send_sem=send_sem, recv_sem=recv_sem, device_id=(device,), device_id_type=MESH,
    ).start()


def iota(shape, axis):
    return lax.broadcasted_iota(jnp.int32, shape, axis)


def running_count(chosen):
    lane = iota(chosen.shape, 1)
    count = chosen.astype(jnp.int32)
    for step in (1, 2, 4, 8, 16, 32, 64):
        count = count + jnp.where(lane >= step, pltpu.roll(count, step, 1), 0)
    return count


def swap_bits(rows, unit, steps):
    lane = iota(rows[0].shape, 1)
    rows = list(rows)
    for step in steps:
        high = (lane & (unit * step)) != 0
        for at in range(len(rows)):
            if at & step:
                continue
            low_row, high_row = rows[at], rows[at + step]
            crossed = jnp.where(high, low_row, high_row)
            if unit * step == 64:
                crossed = pltpu.roll(crossed, 64, 1)
            else:
                crossed = jnp.take_along_axis(crossed, lane ^ (unit * step), axis=1, mode="promise_in_bounds")
            rows[at] = jnp.where(high, crossed, low_row)
            rows[at + step] = jnp.where(high, high_row, crossed)
    return rows


def kernel(state, old_map, new_map, new_lanes, box_level, ghost_list, coupling, out,
           rest, send_ar, recv_a, recv_ar, rolled, send_b, send_br, recv_br, cells, src_v, src_s,
           old_s, new_s, level_s, ghost_s, mix_s, new_v, face_code, level_v, table_v, table_s,
           planes, outbox, inbox, inbox_last, raw, raw_far, faces,
           load_sem, send_sem, recv_sem, small_sem, far_send, far_recv):
    me = lax.axis_index("boxes")
    barrier = pltpu.get_barrier_semaphore()

    def greet(k, c):
        pl.semaphore_signal(barrier, inc=1, device_id=(partner(me, k),), device_id_type=MESH)
        return c

    lax.fori_loop(1, N, greet, 0)
    loads = [
        pltpu.make_async_copy(state.at[4], rest, load_sem.at[0]),
        pltpu.make_async_copy(old_map, old_s, load_sem.at[1]),
        pltpu.make_async_copy(new_map, new_s, load_sem.at[2]),
        pltpu.make_async_copy(new_lanes, new_v, load_sem.at[3]),
        pltpu.make_async_copy(box_level, level_s, load_sem.at[4]),
        pltpu.make_async_copy(ghost_list, ghost_s, load_sem.at[5]),
        pltpu.make_async_copy(coupling, mix_s, load_sem.at[6]),
    ]
    for load in loads:
        load.start()

    def piece(m):
        return state.at[m // 32, :, pl.ds(pl.multiple_of(lax.rem(m, 32) * 128, 128), 128)]

    own = pltpu.make_async_copy(piece(me), recv_a.at[me], load_sem.at[7])
    own.start()
    pl.semaphore_wait(barrier, N - 1)

    def scatter(k, c):
        m = partner(me, k)
        put(piece(m), recv_a.at[me], send_sem.at[0], recv_sem.at[0], m)
        return c

    lax.fori_loop(1, N, scatter, 0)
    loads[0].wait()

    def pack_rest(r, c):
        tile = rest[:, pl.ds(pl.multiple_of(r * 128, 128), 128)]
        for q in range(4):
            send_ar[r * 4 + q] = jnp.concatenate(
                [tile[4 * b:4 * b + 4, 32 * q:32 * q + 32] for b in range(4)], axis=1)
        return c

    lax.fori_loop(0, 32, pack_rest, 0)

    def scatter_rest(k, c):
        m = partner(me, k)
        put(send_ar.at[m], recv_ar.at[me], send_sem.at[1], recv_sem.at[1], m)
        return c

    lax.fori_loop(1, N, scatter_rest, 0)
    recv_ar[me] = send_ar[me]
    for load in loads[1:]:
        load.wait()

    wanted = new_v[...]

    def find(s, c):
        return jnp.where(wanted == old_s[s], s, c)

    source = lax.fori_loop(0, 2048, find, jnp.zeros((16, 128), jnp.int32), unroll=8)
    lane = iota((16, 128), 1)
    turn = (lane // 4 - source // 4 + 8) % 4
    src_v[0:16] = source
    src_v[16:32] = turn * 512 + source // 16 * 4 + source % 4
    to_scalars = pltpu.make_async_copy(src_v, src_s, small_sem.at[0])
    to_scalars.start()

    row8, lane8 = iota((8, 128), 0), iota((8, 128), 1)
    row16 = iota((16, 128), 0)
    nothing = jnp.full((8, 128), -1, jnp.int32)
    zeros16 = jnp.zeros((16, 128), jnp.int32)

    def read_wishes(k, c):
        theirs, their_plane, ours, our_plane, level_here, codes = c
        for at, distance in enumerate(DISTANCES):
            b = new_s[lax.rem(me + distance + N, N) * BOXES + k]
            for f in range(6):
                here = (row8 == at) & (lane8 == f * 16 + k)
                theirs = jnp.where(here, ghost_s[f, 0, b], theirs)
                their_plane = jnp.where(here, ghost_s[f, 1, b], their_plane)
        b = new_s[me * BOXES + k]
        level = level_s[b]
        level_here = jnp.where(row16 == k, level, level_here)
        new_codes = []
        for f in range(6):
            here = lane8 == f * 16 + k
            g = ghost_s[f, 0, b]
            ours = jnp.where(here, g, ours)
            our_plane = jnp.where(here, ghost_s[f, 1, b], our_plane)
            coarser = (level_s[jnp.maximum(g, 0)] < level).astype(jnp.int32)
            code = ghost_s[f, 2, b] // 8 + ghost_s[f, 3, b] // 8 * 2 + coarser * 4
            new_codes.append(jnp.where(row16 == k, code, codes[f]))
        return theirs, their_plane, ours, our_plane, level_here, tuple(new_codes)

    theirs, their_plane, ours, our_plane, level_here, codes = lax.fori_loop(
        0, BOXES, read_wishes, (nothing, nothing, nothing, nothing, zeros16, (zeros16,) * 6))
    level_v[...] = level_here
    for f in range(6):
        face_code[f] = codes[f]

    def find_theirs(t, c):
        return jnp.where(theirs == new_s[me * BOXES + t], t, c)

    their_slot = lax.fori_loop(0, BOXES, find_theirs, nothing)

    def find_ours(t, c):
        return jnp.where(ours == new_s[lax.rem((me - 2 + N) * BOXES + t, N * BOXES)], t, c)

    our_slot = lax.fori_loop(0, 5 * BOXES, find_ours, nothing)
    axis = lane8 // 32
    chosen = their_slot >= 0
    count = running_count(chosen)
    base = (axis * 16 + their_plane) * BLOCK + their_slot
    table = jnp.zeros((8, 128), jnp.int32)
    for j in range(ROOM):
        first = jnp.sum(jnp.where(chosen & (count == j + 1), base, 0), axis=1, keepdims=True)
        table = jnp.where(lane8 == j, first, table)
    low = jnp.where(row8 == 4, 32, 0)
    for at, distance in enumerate(DISTANCES):
        low = jnp.where(row8 == at, 16 * (distance + 2), low)
    chosen = (our_slot >= low) & (our_slot < low + 16) & (row8 < 5)
    count = running_count(chosen)
    for row, count_of in ((4, 8), (6, 2)):
        pitch = count_of * ROWS
        far_base = jnp.sum(
            jnp.where(chosen & (row8 < 4), row8 * pitch + count - 1 - 4 * pitch, 0), axis=0, keepdims=True)
        table = jnp.where(row8 == row, far_base + 4 * pitch, table)
    near_base = jnp.sum(
        jnp.where(chosen & (row8 == 4), (axis * 16 + our_plane) * BLOCK + our_slot - 32 - 48 * BLOCK, 0),
        axis=0, keepdims=True)
    table = jnp.where(row8 == 5, near_base + 48 * BLOCK, table)
    table_v[...] = table
    to_table = pltpu.make_async_copy(table_v, table_s, small_sem.at[1])
    to_table.start()
    planes[48] = jnp.zeros((10, BOXES, 128), jnp.float32)
    inbox[4] = jnp.zeros((8, ROWS, 128), jnp.float32)
    inbox_last[4] = jnp.zeros((2, ROWS, 128), jnp.float32)
    for f in range(5):
        for edge in (0, 1, 34, 35):
            cells[f * PITCH + edge] = jnp.zeros((BOXES, 128), jnp.float32)
    to_scalars.wait()
    to_table.wait()

    own.wait()
    bytes_of(recv_a.at[pl.ds(0, N - 1)], recv_sem.at[0]).wait()
    arrived = recv_a.reshape(2048, 128)
    landing = me // 32 * PITCH + 2 + lax.rem(me, 32)

    def gather(d, into):
        hi = d // 8
        lo = lax.rem(d, 8) * 16
        for t in range(16):
            into[pl.ds(t, 1), :] = arrived[pl.ds(src_s[hi, lo + t], 1), :]

    def forward(k, c):
        d = partner(me, k)
        gather(d, send_b.at[d])
        put(send_b.at[d], cells.at[landing], send_sem.at[2], recv_sem.at[2], d)
        return c

    lax.fori_loop(1, N, forward, 0)
    gather(me, cells.at[landing])
    bytes_of(recv_ar.at[pl.ds(0, N - 1)], recv_sem.at[1]).wait()

    def turn_rest(s, c):
        part = recv_ar[pl.ds(s * 4, 4)].reshape(16, 128)
        for t in range(4):
            rolled[pl.ds(pl.multiple_of(t * 512 + s * 16, 16), 16), :] = (
                pltpu.roll(part, 32 * t, 1) if t else part)
        return c

    lax.fori_loop(0, 32, turn_rest, 0)
    lane1 = iota((1, 128), 1)

    def gather_rest(d, into):
        hi = 16 + d // 8
        lo = lax.rem(d, 8) * 16
        for q in range(4):
            part = [rolled[pl.ds(src_s[hi, lo + i * 4 + q], 1), :] for i in range(4)]
            into[pl.ds(q, 1), :] = jnp.where(
                lane1 < 64, jnp.where(lane1 < 32, part[0], part[1]), jnp.where(lane1 < 96, part[2], part[3]))

    def forward_rest(k, c):
        d = partner(me, k)
        gather_rest(d, send_br.at[d])
        put(send_br.at[d], recv_br.at[me], send_sem.at[3], recv_sem.at[3], d)
        return c

    lax.fori_loop(1, N, forward_rest, 0)
    gather_rest(me, recv_br.at[me])
    bytes_of(cells.at[pl.ds(0, N - 1)], recv_sem.at[2]).wait()

    def transpose_planes(at, c):
        f, half, b = at >> 2, (at >> 1) & 1, pl.multiple_of((at & 1) * 8, 8)
        rows = [cells[f * PITCH + 2 + 2 * i + half, pl.ds(b, 8), :] for i in range(16)]
        for i in range(16):
            planes[i, 2 * f + half, pl.ds(b, 8), :] = rows[i]
        for upper in range(2):
            turned = swap_bits(rows[8 * upper:8 * upper + 8], 16, (4, 2, 1))
            for j in range(8):
                planes[16 + 8 * half + j, 2 * f + upper, pl.ds(b, 8), :] = turned[j]
        turned = swap_bits(rows, 1, (8, 4, 2, 1))
        for k in range(16):
            planes[32 + k, 2 * f + half, pl.ds(b, 8), :] = turned[k]
        return c

    plane_rows = planes.reshape(49 * BLOCK, 128)

    def send_planes(first, count, part):
        cut = pl.ds(first, count)
        for at, distance in enumerate(DISTANCES):
            def fill(j, c, at=at):
                base = table_s[at, j]
                for h in range(first, first + count):
                    outbox[at, h, pl.ds(j, 1), :] = plane_rows[pl.ds(base + h * BOXES, 1), :]
                return c

            lax.fori_loop(0, ROOM, fill, 0, unroll=4)
            put(outbox.at[at, cut], (inbox, inbox_last)[part].at[at ^ 1], far_send.at[part, at], far_recv.at[part, at ^ 1],
                lax.rem(me + distance + N, N))

    def take_near(first, count):
        def take(q, c):
            base = table_s[5, q]
            for h in range(first, first + count):
                raw[h, pl.ds(q, 1), :] = plane_rows[pl.ds(base + h * BOXES, 1), :]
            return c

        lax.fori_loop(0, 96, take, 0, unroll=4)

    lane = iota((8, 128), 1)
    third = lane & 15

    def factors(b):
        scale = (2 - level_v[pl.ds(b, 8), :]).astype(jnp.float32)
        return diffusion_number / (scale * scale), advection_number / scale * 0.5

    def step(at, fields):
        i, b = at >> 1, pl.multiple_of((at & 1) * 8, 8)
        spread, drift = factors(b)

        def at_row(f, r):
            return cells[f * PITCH + 2 + r, pl.ds(b, 8), :]

        values = {f: [at_row(f, 2 * i + h) for h in range(2)] for f in fields}
        for half in range(2):
            sums, differences = {}, {}
            for f in fields:
                here, other = values[f][half], values[f][1 - half]
                before, after = at_row(f, 2 * i + half - 2), at_row(f, 2 * i + half + 2)
                total = after + before - 6.0 * here
                moves = [after - before]
                if half == 0:
                    before = jnp.where(lane < 16, 0.0, pltpu.roll(here, 16, 1))
                    after = pltpu.roll(jnp.where(lane < 16, other, here), 112, 1)
                else:
                    before = pltpu.roll(jnp.where(lane >= 112, other, here), 16, 1)
                    after = jnp.where(lane >= 112, 0.0, pltpu.roll(here, 112, 1))
                total = total + (after + before)
                moves.append(after - before)
                before = jnp.where(third == 0, 0.0, pltpu.roll(here, 1, 1))
                after = jnp.where(third == 15, 0.0, pltpu.roll(here, 127, 1))
                total = total + (after + before)
                moves.append(after - before)
                sums[f] = total
                differences[f] = [drift * move for move in moves]
            for g in range(5):
                value = None
                if 0 not in fields:
                    value = out[g, pl.ds(b, 8), pl.ds(pl.multiple_of((2 * i + half) * 128, 128), 128)]
                if g in fields:
                    own = values[g][half] + spread * sums[g]
                    value = own if value is None else value + own
                for a in range(3):
                    for f in fields:
                        term = mix_s[g, a, f] * differences[f][a]
                        value = -term if value is None else value - term
                out[g, pl.ds(b, 8), pl.ds(pl.multiple_of((2 * i + half) * 128, 128), 128)] = value

    def step_four(at, c):
        step(at, (0, 1, 2, 3))
        return c

    def step_last(at, c):
        step(at, (4,))
        return c

    lax.fori_loop(0, 16, transpose_planes, 0, unroll=2)
    send_planes(0, 8, 0)
    take_near(0, 8)
    lax.fori_loop(0, EARLY, step_four, 0, unroll=2)

    bytes_of(recv_br.at[pl.ds(0, N - 1)], recv_sem.at[3]).wait()

    def unpack_rest(r, c):
        parts = [recv_br[pl.ds(r * 32 + q, 8, stride=4)].reshape(32, 128) for q in range(4)]
        for b, part in enumerate(swap_bits(parts, 32, (2, 1))):
            cells[pl.ds(4 * PITCH + 2 + 8 * r, 8), 4 * b:4 * b + 4, :] = part.reshape(8, 4, 128)
        return c

    lax.fori_loop(0, 4, unpack_rest, 0)
    lax.fori_loop(16, 20, transpose_planes, 0, unroll=2)
    send_planes(8, 2, 1)
    take_near(8, 2)
    lax.fori_loop(EARLY, 32, step_four, 0, unroll=2)
    lax.fori_loop(0, 32, step_last, 0, unroll=4)

    def add_face(face, part, fields):
        b = pl.multiple_of(part * 8, 8)
        spread, drift = factors(b)
        code = face_code[face, pl.ds(b, 8), :]
        coarse = code >= 4
        first, second = code & 1, (code >> 1) & 1
        if face >= 4:
            first, second = second, first
        low_first = coarse & (first == 0)
        high_first = coarse & (first == 1)
        fine_pick = ((lane >> 5) << 4) + second * 8 + ((lane & 15) >> 1)
        picks = [jnp.where(coarse, 64 * half + fine_pick, lane) for half in range(2)]
        sign = drift if face % 2 == 0 else -drift
        ghost = {}
        for f in fields:
            rows = pl.ds(16 * face + b, 8)
            half = [raw[2 * f + h, rows, :] + raw_far[2 * f + h, rows, :] for h in range(2)]
            chosen = [jnp.where(high_first, half[1], half[0]), jnp.where(low_first, half[0], half[1])]
            ghost[f] = [
                jnp.take_along_axis(chosen[h], picks[h], axis=1, mode="promise_in_bounds") for h in range(2)]
        for g in range(5):
            for h in range(2):
                flux = None
                for f in fields:
                    term = mix_s[g, face // 2, f] * ghost[f][h]
                    flux = term if flux is None else flux + term
                value = sign * flux
                if g in fields:
                    value = value + spread * ghost[g][h]
                if face < 2:
                    at = (30 * face + h) * 128
                    out[g, pl.ds(b, 8), at:at + 128] = out[g, pl.ds(b, 8), at:at + 128] + value
                elif 0 in fields:
                    faces[face - 2, 2 * g + h, pl.ds(b, 8), :] = value
                else:
                    faces[face - 2, 2 * g + h, pl.ds(b, 8), :] = (
                        faces[face - 2, 2 * g + h, pl.ds(b, 8), :] + value)

    def add_planes(first, count, part, fields):
        landed = (inbox, inbox_last)[part]
        for at in range(4):
            bytes_of(landed.at[at], far_recv.at[part, at]).wait()
        landed_rows = landed.reshape(5 * count * ROWS, 128)

        def take(q, c):
            base = table_s[4 + 2 * part, q]
            for h in range(count):
                raw_far[first + h, pl.ds(q, 1), :] = landed_rows[pl.ds(base + h * ROWS, 1), :]
            return c

        lax.fori_loop(0, 96, take, 0, unroll=4)
        for face in range(6):
            def add(part, c, face=face):
                add_face(face, part, fields)
                return c

            lax.fori_loop(0, 2, add, 0, unroll=2)

    add_planes(0, 8, 0, (0, 1, 2, 3))
    add_planes(8, 2, 1, (4,))

    def spread_faces(at, c):
        g, b = at >> 1, pl.multiple_of((at & 1) * 8, 8)
        halves = [[faces[f, 2 * g + h, pl.ds(b, 8), :] for h in range(2)] for f in range(4)]
        after_second = [pltpu.roll(v, 112, 1) for v in halves[1]]
        after_third = [pltpu.roll(v, 15, 1) for v in halves[3]]
        for i in range(16):
            both = jnp.where(lane >> 4 == i % 8, halves[0][i // 8], after_second[i // 8])
            edge = pltpu.roll(both, (128 - 16 * (i % 8)) % 128, 1) if i % 8 else both
            edges = (jnp.where(lane < 16, edge, 0.0), jnp.where(lane >= 112, edge, 0.0))
            for half in range(2):
                cut = slice((2 * i + half) * 128, (2 * i + half + 1) * 128)
                both = jnp.where(third == i, halves[2][half], after_third[half])
                both = pltpu.roll(both, 128 - i, 1) if i else both
                value = jnp.where((third == 0) | (third == 15), both, 0.0)
                out[g, pl.ds(b, 8), cut] = out[g, pl.ds(b, 8), cut] + (value + edges[half])
        return c

    lax.fori_loop(0, 10, spread_faces, 0, unroll=2)
    bytes_of(recv_a.at[pl.ds(0, N - 1)], send_sem.at[0]).wait()
    for at, ref in ((1, send_ar), (2, send_b), (3, send_br)):
        bytes_of(ref.at[pl.ds(0, N - 1)], send_sem.at[at]).wait()
    for part, cut in enumerate((pl.ds(0, 8), pl.ds(8, 2))):
        for at in range(4):
            bytes_of(outbox.at[at, cut], far_send.at[part, at]).wait()


def shards(old_state, old_map, new_map, box_level, ghost_list, coupling):
    vmem = pl.BlockSpec(memory_space=pltpu.VMEM)
    hbm = pl.BlockSpec(memory_space=pltpu.HBM)
    f32, i32 = jnp.float32, jnp.int32
    dma = pltpu.SemaphoreType.DMA
    stepped = pl.pallas_call(
        kernel,
        out_shape=jax.ShapeDtypeStruct((5, BOXES, 4096), f32),
        in_specs=[hbm] * 7,
        out_specs=vmem,
        scratch_shapes=[
            pltpu.VMEM((BOXES, 4096), f32),
            pltpu.VMEM((N, 4, 128), f32),
            pltpu.VMEM((N, BOXES, 128), f32),
            pltpu.VMEM((N, 4, 128), f32),
            pltpu.VMEM((2048, 128), f32),
            pltpu.VMEM((N, BOXES, 128), f32),
            pltpu.VMEM((N, 4, 128), f32),
            pltpu.VMEM((N, 4, 128), f32),
            pltpu.VMEM((5 * PITCH, BOXES, 128), f32),
            pltpu.VMEM((32, 128), i32),
            pltpu.SMEM((32, 128), i32),
            pltpu.SMEM((2048,), i32),
            pltpu.SMEM((2048,), i32),
            pltpu.SMEM((2048,), i32),
            pltpu.SMEM((6, 4, 2048), i32),
            pltpu.SMEM((5, 3, 5), f32),
            pltpu.VMEM((16, 128), i32),
            pltpu.VMEM((6, 16, 128), i32),
            pltpu.VMEM((16, 128), i32),
            pltpu.VMEM((8, 128), i32),
            pltpu.SMEM((8, 128), i32),
            pltpu.VMEM((49, 10, BOXES, 128), f32),
            pltpu.VMEM((4, 10, ROWS, 128), f32),
            pltpu.VMEM((5, 8, ROWS, 128), f32),
            pltpu.VMEM((5, 2, ROWS, 128), f32),
            pltpu.VMEM((10, 96, 128), f32),
            pltpu.VMEM((10, 96, 128), f32),
            pltpu.VMEM((4, 10, BOXES, 128), f32),
            dma((8,)),
            dma((4,)),
            dma((4,)),
            dma((2,)),
            dma((2, 4)),
            dma((2, 4)),
        ],
        compiler_params=pltpu.CompilerParams(
            collective_id=0, has_side_effects=True, vmem_limit_bytes=48 << 20),
    )(
        old_state.transpose(1, 0, 2), old_map, new_map, new_map.reshape(16, 128), box_level,
        ghost_list.transpose(1, 2, 0), coupling.transpose(1, 0, 2),
    )
    return stepped.transpose(1, 0, 2)


def solution(mesh):
    return jax.shard_map(
        shards,
        mesh=mesh,
        in_specs=(P("boxes", None, None), P(), P(), P(), P(), P()),
        out_specs=P("boxes", None, None),
        check_vma=False,
    )
```

```python
import jax
import jax.numpy as jnp
from jax import lax
from jax.experimental import pallas as pl
from jax.experimental.pallas import tpu as pltpu
from jax.sharding import PartitionSpec as P

MESH = pl.DeviceIdType.MESH
N = 128
BOXES = 16
STRIDE = 27
DISTANCES = (-2, 2, -1, 1)
ROOM = 20
ROWS = 24
PITCH = 36
BLOCK = 10 * BOXES
EARLY = 12
diffusion_number = 0.12
advection_number = 0.25


def partner(me, k):
    return lax.rem(me + k * STRIDE, N)


def bytes_of(ref, sem):
    return pltpu.make_async_copy(ref, ref, sem)


def put(src, dst, send_sem, recv_sem, device):
    pltpu.make_async_remote_copy(
        src_ref=src, dst_ref=dst, send_sem=send_sem, recv_sem=recv_sem, device_id=(device,), device_id_type=MESH,
    ).start()


def iota(shape, axis):
    return lax.broadcasted_iota(jnp.int32, shape, axis)


def running_count(chosen):
    lane = iota(chosen.shape, 1)
    count = chosen.astype(jnp.int32)
    for step in (1, 2, 4, 8, 16, 32, 64):
        count = count + jnp.where(lane >= step, pltpu.roll(count, step, 1), 0)
    return count


def swap_bits(rows, unit, steps):
    lane = iota(rows[0].shape, 1)
    rows = list(rows)
    for step in steps:
        high = (lane & (unit * step)) != 0
        for at in range(len(rows)):
            if at & step:
                continue
            low_row, high_row = rows[at], rows[at + step]
            crossed = jnp.where(high, low_row, high_row)
            if unit * step == 64:
                crossed = pltpu.roll(crossed, 64, 1)
            else:
                crossed = jnp.take_along_axis(crossed, lane ^ (unit * step), axis=1, mode="promise_in_bounds")
            rows[at] = jnp.where(high, crossed, low_row)
            rows[at + step] = jnp.where(high, high_row, crossed)
    return rows


def kernel(state, old_map, new_map, new_lanes, box_level, ghost_list, coupling, out,
           rest, send_ar, recv_a, recv_ar, rolled, send_b, send_br, recv_br, cells, src_v, src_s,
           old_s, new_s, level_s, ghost_s, mix_s, new_v, face_code, level_v, table_v, table_s,
           planes, outbox, inbox, inbox_last, raw, raw_far, faces,
           load_sem, send_sem, recv_sem, small_sem, far_send, far_recv):
    me = lax.axis_index("boxes")
    barrier = pltpu.get_barrier_semaphore()

    def greet(k, c):
        pl.semaphore_signal(barrier, inc=1, device_id=(partner(me, k),), device_id_type=MESH)
        return c

    lax.fori_loop(1, N, greet, 0)
    loads = [
        pltpu.make_async_copy(state.at[4], rest, load_sem.at[0]),
        pltpu.make_async_copy(old_map, old_s, load_sem.at[1]),
        pltpu.make_async_copy(new_map, new_s, load_sem.at[2]),
        pltpu.make_async_copy(new_lanes, new_v, load_sem.at[3]),
        pltpu.make_async_copy(box_level, level_s, load_sem.at[4]),
        pltpu.make_async_copy(ghost_list, ghost_s, load_sem.at[5]),
        pltpu.make_async_copy(coupling, mix_s, load_sem.at[6]),
    ]
    for load in loads:
        load.start()

    def piece(m):
        return state.at[m // 32, :, pl.ds(pl.multiple_of(lax.rem(m, 32) * 128, 128), 128)]

    own = pltpu.make_async_copy(piece(me), recv_a.at[me], load_sem.at[7])
    own.start()
    pl.semaphore_wait(barrier, N - 1)

    def scatter(k, c):
        m = partner(me, k)
        put(piece(m), recv_a.at[me], send_sem.at[0], recv_sem.at[0], m)
        return c

    lax.fori_loop(1, N, scatter, 0)
    loads[0].wait()

    def pack_rest(r, c):
        tile = rest[:, pl.ds(pl.multiple_of(r * 128, 128), 128)]
        for q in range(4):
            send_ar[r * 4 + q] = jnp.concatenate(
                [tile[4 * b:4 * b + 4, 32 * q:32 * q + 32] for b in range(4)], axis=1)
        return c

    lax.fori_loop(0, 32, pack_rest, 0)

    def scatter_rest(k, c):
        m = partner(me, k)
        put(send_ar.at[m], recv_ar.at[me], send_sem.at[1], recv_sem.at[1], m)
        return c

    lax.fori_loop(1, N, scatter_rest, 0)
    recv_ar[me] = send_ar[me]
    for load in loads[1:]:
        load.wait()

    wanted = new_v[...]

    def find(s, c):
        return jnp.where(wanted == old_s[s], s, c)

    source = lax.fori_loop(0, 2048, find, jnp.zeros((16, 128), jnp.int32), unroll=8)
    lane = iota((16, 128), 1)
    turn = (lane // 4 - source // 4 + 8) % 4
    src_v[0:16] = source
    src_v[16:32] = turn * 512 + source // 16 * 4 + source % 4
    to_scalars = pltpu.make_async_copy(src_v, src_s, small_sem.at[0])
    to_scalars.start()

    row8, lane8 = iota((8, 128), 0), iota((8, 128), 1)
    row16 = iota((16, 128), 0)
    nothing = jnp.full((8, 128), -1, jnp.int32)
    zeros16 = jnp.zeros((16, 128), jnp.int32)

    def read_wishes(k, c):
        theirs, their_plane, ours, our_plane, level_here, codes = c
        for at, distance in enumerate(DISTANCES):
            b = new_s[lax.rem(me + distance + N, N) * BOXES + k]
            for f in range(6):
                here = (row8 == at) & (lane8 == f * 16 + k)
                theirs = jnp.where(here, ghost_s[f, 0, b], theirs)
                their_plane = jnp.where(here, ghost_s[f, 1, b], their_plane)
        b = new_s[me * BOXES + k]
        level = level_s[b]
        level_here = jnp.where(row16 == k, level, level_here)
        new_codes = []
        for f in range(6):
            here = lane8 == f * 16 + k
            g = ghost_s[f, 0, b]
            ours = jnp.where(here, g, ours)
            our_plane = jnp.where(here, ghost_s[f, 1, b], our_plane)
            coarser = (level_s[jnp.maximum(g, 0)] < level).astype(jnp.int32)
            code = ghost_s[f, 2, b] // 8 + ghost_s[f, 3, b] // 8 * 2 + coarser * 4
            new_codes.append(jnp.where(row16 == k, code, codes[f]))
        return theirs, their_plane, ours, our_plane, level_here, tuple(new_codes)

    theirs, their_plane, ours, our_plane, level_here, codes = lax.fori_loop(
        0, BOXES, read_wishes, (nothing, nothing, nothing, nothing, zeros16, (zeros16,) * 6))
    level_v[...] = level_here
    for f in range(6):
        face_code[f] = codes[f]

    def find_theirs(t, c):
        return jnp.where(theirs == new_s[me * BOXES + t], t, c)

    their_slot = lax.fori_loop(0, BOXES, find_theirs, nothing)

    def find_ours(t, c):
        return jnp.where(ours == new_s[lax.rem((me - 2 + N) * BOXES + t, N * BOXES)], t, c)

    our_slot = lax.fori_loop(0, 5 * BOXES, find_ours, nothing)
    axis = lane8 // 32
    chosen = their_slot >= 0
    count = running_count(chosen)
    base = (axis * 16 + their_plane) * BLOCK + their_slot
    table = jnp.zeros((8, 128), jnp.int32)
    for j in range(ROOM):
        first = jnp.sum(jnp.where(chosen & (count == j + 1), base, 0), axis=1, keepdims=True)
        table = jnp.where(lane8 == j, first, table)
    low = jnp.where(row8 == 4, 32, 0)
    for at, distance in enumerate(DISTANCES):
        low = jnp.where(row8 == at, 16 * (distance + 2), low)
    chosen = (our_slot >= low) & (our_slot < low + 16) & (row8 < 5)
    count = running_count(chosen)
    for row, count_of in ((4, 8), (6, 2)):
        pitch = count_of * ROWS
        far_base = jnp.sum(
            jnp.where(chosen & (row8 < 4), row8 * pitch + count - 1 - 4 * pitch, 0), axis=0, keepdims=True)
        table = jnp.where(row8 == row, far_base + 4 * pitch, table)
    near_base = jnp.sum(
        jnp.where(chosen & (row8 == 4), (axis * 16 + our_plane) * BLOCK + our_slot - 32 - 48 * BLOCK, 0),
        axis=0, keepdims=True)
    table = jnp.where(row8 == 5, near_base + 48 * BLOCK, table)
    table_v[...] = table
    to_table = pltpu.make_async_copy(table_v, table_s, small_sem.at[1])
    to_table.start()
    planes[48] = jnp.zeros((10, BOXES, 128), jnp.float32)
    inbox[4] = jnp.zeros((8, ROWS, 128), jnp.float32)
    inbox_last[4] = jnp.zeros((2, ROWS, 128), jnp.float32)
    for f in range(5):
        for edge in (0, 1, 34, 35):
            cells[f * PITCH + edge] = jnp.zeros((BOXES, 128), jnp.float32)
    to_scalars.wait()
    to_table.wait()

    own.wait()
    bytes_of(recv_a.at[pl.ds(0, N - 1)], recv_sem.at[0]).wait()
    arrived = recv_a.reshape(2048, 128)
    landing = me // 32 * PITCH + 2 + lax.rem(me, 32)

    def gather(d, into):
        hi = d // 8
        lo = lax.rem(d, 8) * 16
        for t in range(16):
            into[pl.ds(t, 1), :] = arrived[pl.ds(src_s[hi, lo + t], 1), :]

    def forward(k, c):
        d = partner(me, k)
        gather(d, send_b.at[d])
        put(send_b.at[d], cells.at[landing], send_sem.at[2], recv_sem.at[2], d)
        return c

    lax.fori_loop(1, N, forward, 0, unroll=4)
    gather(me, cells.at[landing])
    bytes_of(recv_ar.at[pl.ds(0, N - 1)], recv_sem.at[1]).wait()

    def turn_rest(s, c):
        part = recv_ar[pl.ds(s * 4, 4)].reshape(16, 128)
        for t in range(4):
            rolled[pl.ds(pl.multiple_of(t * 512 + s * 16, 16), 16), :] = (
                pltpu.roll(part, 32 * t, 1) if t else part)
        return c

    lax.fori_loop(0, 32, turn_rest, 0)
    lane1 = iota((1, 128), 1)

    def gather_rest(d, into):
        hi = 16 + d // 8
        lo = lax.rem(d, 8) * 16
        for q in range(4):
            part = [rolled[pl.ds(src_s[hi, lo + i * 4 + q], 1), :] for i in range(4)]
            into[pl.ds(q, 1), :] = jnp.where(
                lane1 < 64, jnp.where(lane1 < 32, part[0], part[1]), jnp.where(lane1 < 96, part[2], part[3]))

    def forward_rest(k, c):
        d = partner(me, k)
        gather_rest(d, send_br.at[d])
        put(send_br.at[d], recv_br.at[me], send_sem.at[3], recv_sem.at[3], d)
        return c

    lax.fori_loop(1, N, forward_rest, 0, unroll=4)
    gather_rest(me, recv_br.at[me])
    bytes_of(cells.at[pl.ds(0, N - 1)], recv_sem.at[2]).wait()

    def transpose_planes(at, c):
        f, half, b = at >> 2, (at >> 1) & 1, pl.multiple_of((at & 1) * 8, 8)
        rows = [cells[f * PITCH + 2 + 2 * i + half, pl.ds(b, 8), :] for i in range(16)]
        for i in range(16):
            planes[i, 2 * f + half, pl.ds(b, 8), :] = rows[i]
        for upper in range(2):
            turned = swap_bits(rows[8 * upper:8 * upper + 8], 16, (4, 2, 1))
            for j in range(8):
                planes[16 + 8 * half + j, 2 * f + upper, pl.ds(b, 8), :] = turned[j]
        turned = swap_bits(rows, 1, (8, 4, 2, 1))
        for k in range(16):
            planes[32 + k, 2 * f + half, pl.ds(b, 8), :] = turned[k]
        return c

    plane_rows = planes.reshape(49 * BLOCK, 128)

    def send_planes(first, count, part):
        cut = pl.ds(first, count)
        for at, distance in enumerate(DISTANCES):
            def fill(j, c, at=at):
                base = table_s[at, j]
                for h in range(first, first + count):
                    outbox[at, h, pl.ds(j, 1), :] = plane_rows[pl.ds(base + h * BOXES, 1), :]
                return c

            lax.fori_loop(0, ROOM, fill, 0, unroll=4)
            put(outbox.at[at, cut], (inbox, inbox_last)[part].at[at ^ 1], far_send.at[part, at], far_recv.at[part, at ^ 1],
                lax.rem(me + distance + N, N))

    def take_near(first, count):
        def take(q, c):
            base = table_s[5, q]
            for h in range(first, first + count):
                raw[h, pl.ds(q, 1), :] = plane_rows[pl.ds(base + h * BOXES, 1), :]
            return c

        lax.fori_loop(0, 96, take, 0, unroll=4)

    lane = iota((8, 128), 1)
    third = lane & 15

    def factors(b):
        scale = (2 - level_v[pl.ds(b, 8), :]).astype(jnp.float32)
        return diffusion_number / (scale * scale), advection_number / scale * 0.5

    def step(at, fields):
        i, b = at >> 1, pl.multiple_of((at & 1) * 8, 8)
        spread, drift = factors(b)

        def at_row(f, r):
            return cells[f * PITCH + 2 + r, pl.ds(b, 8), :]

        values = {f: [at_row(f, 2 * i + h) for h in range(2)] for f in fields}
        for half in range(2):
            sums, differences = {}, {}
            for f in fields:
                here, other = values[f][half], values[f][1 - half]
                before, after = at_row(f, 2 * i + half - 2), at_row(f, 2 * i + half + 2)
                total = after + before - 6.0 * here
                moves = [after - before]
                if half == 0:
                    before = jnp.where(lane < 16, 0.0, pltpu.roll(here, 16, 1))
                    after = pltpu.roll(jnp.where(lane < 16, other, here), 112, 1)
                else:
                    before = pltpu.roll(jnp.where(lane >= 112, other, here), 16, 1)
                    after = jnp.where(lane >= 112, 0.0, pltpu.roll(here, 112, 1))
                total = total + (after + before)
                moves.append(after - before)
                before = jnp.where(third == 0, 0.0, pltpu.roll(here, 1, 1))
                after = jnp.where(third == 15, 0.0, pltpu.roll(here, 127, 1))
                total = total + (after + before)
                moves.append(after - before)
                sums[f] = total
                differences[f] = [drift * move for move in moves]
            for g in range(5):
                value = None
                if 0 not in fields:
                    value = out[g, pl.ds(b, 8), pl.ds(pl.multiple_of((2 * i + half) * 128, 128), 128)]
                if g in fields:
                    own = values[g][half] + spread * sums[g]
                    value = own if value is None else value + own
                for a in range(3):
                    for f in fields:
                        term = mix_s[g, a, f] * differences[f][a]
                        value = -term if value is None else value - term
                out[g, pl.ds(b, 8), pl.ds(pl.multiple_of((2 * i + half) * 128, 128), 128)] = value

    def step_four(at, c):
        step(at, (0, 1, 2, 3))
        return c

    def step_last(at, c):
        step(at, (4,))
        return c

    lax.fori_loop(0, 16, transpose_planes, 0, unroll=2)
    send_planes(0, 8, 0)
    take_near(0, 8)
    lax.fori_loop(0, EARLY, step_four, 0, unroll=2)

    bytes_of(recv_br.at[pl.ds(0, N - 1)], recv_sem.at[3]).wait()

    def unpack_rest(r, c):
        parts = [recv_br[pl.ds(r * 32 + q, 8, stride=4)].reshape(32, 128) for q in range(4)]
        for b, part in enumerate(swap_bits(parts, 32, (2, 1))):
            cells[pl.ds(4 * PITCH + 2 + 8 * r, 8), 4 * b:4 * b + 4, :] = part.reshape(8, 4, 128)
        return c

    lax.fori_loop(0, 4, unpack_rest, 0)
    lax.fori_loop(16, 20, transpose_planes, 0, unroll=2)
    send_planes(8, 2, 1)
    take_near(8, 2)
    lax.fori_loop(EARLY, 32, step_four, 0, unroll=2)
    lax.fori_loop(0, 32, step_last, 0, unroll=4)

    def add_face(face, part, fields):
        b = pl.multiple_of(part * 8, 8)
        spread, drift = factors(b)
        code = face_code[face, pl.ds(b, 8), :]
        coarse = code >= 4
        first, second = code & 1, (code >> 1) & 1
        if face >= 4:
            first, second = second, first
        low_first = coarse & (first == 0)
        high_first = coarse & (first == 1)
        fine_pick = ((lane >> 5) << 4) + second * 8 + ((lane & 15) >> 1)
        picks = [jnp.where(coarse, 64 * half + fine_pick, lane) for half in range(2)]
        sign = drift if face % 2 == 0 else -drift
        ghost = {}
        for f in fields:
            rows = pl.ds(16 * face + b, 8)
            half = [raw[2 * f + h, rows, :] + raw_far[2 * f + h, rows, :] for h in range(2)]
            chosen = [jnp.where(high_first, half[1], half[0]), jnp.where(low_first, half[0], half[1])]
            ghost[f] = [
                jnp.take_along_axis(chosen[h], picks[h], axis=1, mode="promise_in_bounds") for h in range(2)]
        for g in range(5):
            for h in range(2):
                flux = None
                for f in fields:
                    term = mix_s[g, face // 2, f] * ghost[f][h]
                    flux = term if flux is None else flux + term
                value = sign * flux
                if g in fields:
                    value = value + spread * ghost[g][h]
                if face < 2:
                    at = (30 * face + h) * 128
                    out[g, pl.ds(b, 8), at:at + 128] = out[g, pl.ds(b, 8), at:at + 128] + value
                elif 0 in fields:
                    faces[face - 2, 2 * g + h, pl.ds(b, 8), :] = value
                else:
                    faces[face - 2, 2 * g + h, pl.ds(b, 8), :] = (
                        faces[face - 2, 2 * g + h, pl.ds(b, 8), :] + value)

    def add_planes(first, count, part, fields):
        landed = (inbox, inbox_last)[part]
        for at in range(4):
            bytes_of(landed.at[at], far_recv.at[part, at]).wait()
        landed_rows = landed.reshape(5 * count * ROWS, 128)

        def take(q, c):
            base = table_s[4 + 2 * part, q]
            for h in range(count):
                raw_far[first + h, pl.ds(q, 1), :] = landed_rows[pl.ds(base + h * ROWS, 1), :]
            return c

        lax.fori_loop(0, 96, take, 0, unroll=4)
        for face in range(6):
            def add(part, c, face=face):
                add_face(face, part, fields)
                return c

            lax.fori_loop(0, 2, add, 0, unroll=2)

    add_planes(0, 8, 0, (0, 1, 2, 3))
    add_planes(8, 2, 1, (4,))

    def spread_faces(at, c):
        g, b = at >> 1, pl.multiple_of((at & 1) * 8, 8)
        halves = [[faces[f, 2 * g + h, pl.ds(b, 8), :] for h in range(2)] for f in range(4)]
        after_second = [pltpu.roll(v, 112, 1) for v in halves[1]]
        after_third = [pltpu.roll(v, 15, 1) for v in halves[3]]
        for i in range(16):
            both = jnp.where(lane >> 4 == i % 8, halves[0][i // 8], after_second[i // 8])
            edge = pltpu.roll(both, (128 - 16 * (i % 8)) % 128, 1) if i % 8 else both
            edges = (jnp.where(lane < 16, edge, 0.0), jnp.where(lane >= 112, edge, 0.0))
            for half in range(2):
                cut = slice((2 * i + half) * 128, (2 * i + half + 1) * 128)
                both = jnp.where(third == i, halves[2][half], after_third[half])
                both = pltpu.roll(both, 128 - i, 1) if i else both
                value = jnp.where((third == 0) | (third == 15), both, 0.0)
                out[g, pl.ds(b, 8), cut] = out[g, pl.ds(b, 8), cut] + (value + edges[half])
        return c

    lax.fori_loop(0, 10, spread_faces, 0, unroll=2)
    bytes_of(recv_a.at[pl.ds(0, N - 1)], send_sem.at[0]).wait()
    for at, ref in ((1, send_ar), (2, send_b), (3, send_br)):
        bytes_of(ref.at[pl.ds(0, N - 1)], send_sem.at[at]).wait()
    for part, cut in enumerate((pl.ds(0, 8), pl.ds(8, 2))):
        for at in range(4):
            bytes_of(outbox.at[at, cut], far_send.at[part, at]).wait()


def shards(old_state, old_map, new_map, box_level, ghost_list, coupling):
    vmem = pl.BlockSpec(memory_space=pltpu.VMEM)
    hbm = pl.BlockSpec(memory_space=pltpu.HBM)
    f32, i32 = jnp.float32, jnp.int32
    dma = pltpu.SemaphoreType.DMA
    stepped = pl.pallas_call(
        kernel,
        out_shape=jax.ShapeDtypeStruct((5, BOXES, 4096), f32),
        in_specs=[hbm] * 7,
        out_specs=vmem,
        scratch_shapes=[
            pltpu.VMEM((BOXES, 4096), f32),
            pltpu.VMEM((N, 4, 128), f32),
            pltpu.VMEM((N, BOXES, 128), f32),
            pltpu.VMEM((N, 4, 128), f32),
            pltpu.VMEM((2048, 128), f32),
            pltpu.VMEM((N, BOXES, 128), f32),
            pltpu.VMEM((N, 4, 128), f32),
            pltpu.VMEM((N, 4, 128), f32),
            pltpu.VMEM((5 * PITCH, BOXES, 128), f32),
            pltpu.VMEM((32, 128), i32),
            pltpu.SMEM((32, 128), i32),
            pltpu.SMEM((2048,), i32),
            pltpu.SMEM((2048,), i32),
            pltpu.SMEM((2048,), i32),
            pltpu.SMEM((6, 4, 2048), i32),
            pltpu.SMEM((5, 3, 5), f32),
            pltpu.VMEM((16, 128), i32),
            pltpu.VMEM((6, 16, 128), i32),
            pltpu.VMEM((16, 128), i32),
            pltpu.VMEM((8, 128), i32),
            pltpu.SMEM((8, 128), i32),
            pltpu.VMEM((49, 10, BOXES, 128), f32),
            pltpu.VMEM((4, 10, ROWS, 128), f32),
            pltpu.VMEM((5, 8, ROWS, 128), f32),
            pltpu.VMEM((5, 2, ROWS, 128), f32),
            pltpu.VMEM((10, 96, 128), f32),
            pltpu.VMEM((10, 96, 128), f32),
            pltpu.VMEM((4, 10, BOXES, 128), f32),
            dma((8,)),
            dma((4,)),
            dma((4,)),
            dma((2,)),
            dma((2, 4)),
            dma((2, 4)),
        ],
        compiler_params=pltpu.CompilerParams(
            collective_id=0, has_side_effects=True, vmem_limit_bytes=48 << 20),
    )(
        old_state.transpose(1, 0, 2), old_map, new_map, new_map.reshape(16, 128), box_level,
        ghost_list.transpose(1, 2, 0), coupling.transpose(1, 0, 2),
    )
    return stepped.transpose(1, 0, 2)


def solution(mesh):
    return jax.shard_map(
        shards,
        mesh=mesh,
        in_specs=(P("boxes", None, None), P(), P(), P(), P(), P()),
        out_specs=P("boxes", None, None),
        check_vma=False,
    )
```
